32 devices in a mesh: energy: 8 (over z, x), momentum: 4 (over y, core).
Axes of the slice: x: 2, y: 2, z: 4, core: 2. Of those that a mesh axis runs over, the one named last changes fastest.
Arguments:
- green_tiles: bfloat16 [4, 16, 4, 2, 128, 128], P('momentum', 'energy'), may hold values from -6 to 6
- dham_blocks: bfloat16 [3, 4, 2, 128, 128], replicated, may hold values from -0.375 to 0.375
- phonon_weight: float32 [6, 3, 2], replicated, may hold values from 0.1 to 0.5
- phonon_modes: int32 [6, 2], replicated, may hold values from -1 to 2, as said below
- tile_pattern: int32 [4, 2], replicated, may hold values from 0 to 3, as said below
Outputs:
- self_energy: bfloat16 [4, 16, 4, 2, 128, 128], P('momentum', 'energy')
The draws below stay inside these ranges and needn't reach their ends.
Inputs may be any that keep to these rules, and one draw needn't show every extreme that they name: `phonon_modes`: column 0 is a momentum offset and each of -1, 0, 1 is used by some mode; column 1 is an energy offset and each of 1 to 2 is used by some mode. `tile_pattern`: every block number appears in each column.
All inputs are finite; a program needn't handle non-finite values.
Results may differ from the reference program's by a relative error of at most 0.0062.
Values may be sent and summed in bfloat16 or wider, within the bound.
No kernel may reach another device: no remote copies, remote signals or barrier semaphores. Data moves between devices by JAX's collectives and lax.ppermute only.
A program may use at most 64 MiB of HBM per device.

```python
import math
import jax
import jax.numpy as jnp
from jax import lax

TS = 128
NT = 4
NB = 4
NQ = 6
E_DEV = 2
NE = 16
NK = 4


def draw_phonon_modes(key, part):
    first = jax.random.fold_in(key, 11)
    second = jax.random.fold_in(key, 23)
    momentum_steps = jax.random.permutation(first, jnp.arange(NQ, dtype=jnp.int32) % 3) - 1
    energy_steps = jax.random.permutation(second, jnp.arange(NQ, dtype=jnp.int32) % E_DEV) + 1
    return jnp.stack([momentum_steps, energy_steps], axis=1).astype(jnp.int32)


def draw_tile_pattern(key, part):
    first = jax.random.fold_in(key, 37)
    second = jax.random.fold_in(key, 41)
    left_side = jax.random.permutation(first, jnp.arange(NT, dtype=jnp.int32) % NB)
    right_side = jax.random.permutation(second, jnp.arange(NT, dtype=jnp.int32) % NB)
    return jnp.stack([left_side, right_side], axis=1).astype(jnp.int32)


def block_scale(own_key, shape, pieces, low, largest):
    loudness, own = 1.0, jax.random.fold_in(own_key, 6)
    for axis_at, blocks in pieces:
        steps = jnp.exp(jax.random.uniform(jax.random.fold_in(own, axis_at), (blocks,), jnp.float32, low / len(pieces), largest / len(pieces)))
        loudness = loudness * jnp.repeat(steps, shape[axis_at] // blocks).reshape([-1 if axis == axis_at else 1 for axis in range(len(shape))])
    return loudness


def centred(rng, dims, spread, reach, pieces=(), held_as=jnp.bfloat16):
    result = spread * jax.random.normal(rng, dims, jnp.float32)
    if pieces:
        result = result * block_scale(rng, dims, pieces, -0.22, 0.18)
    return jnp.clip(result, -reach, reach).astype(held_as)


def setup_inputs(seed: int = 0) -> dict:
    splits = jax.random.split(jax.random.key(seed), 6)
    green_tiles = centred(splits[0], (NK, NE, NT, 2, TS, TS), 1.0, 6.0, ((0, 4), (1, 8)))
    dham_blocks = centred(splits[1], (3, NB, 2, TS, TS), (2 * TS) ** -0.5, 0.375)
    phonon_weight = jnp.clip(jnp.exp(jax.random.uniform(splits[2], (NQ, 3, 2), jnp.float32, math.log(0.1), math.log(0.5))), 0.1, 0.5)
    phonon_modes = draw_phonon_modes(jax.random.fold_in(splits[5], 71), 0)
    tile_pattern = draw_tile_pattern(jax.random.fold_in(splits[5], 71), 0)
    return {"green_tiles": green_tiles, "dham_blocks": dham_blocks, "phonon_weight": phonon_weight, "phonon_modes": phonon_modes, "tile_pattern": tile_pattern}


OFFSETS = (-1, 0, 1)


def stack_blocks(left_sel, right_sel):
    left_real = left_sel[:, :, 0]
    left_imag = left_sel[:, :, 1]
    upper_row = jnp.stack([left_real, -left_imag], axis=3)
    lower_row = jnp.stack([left_imag, left_real], axis=3)
    left_big = jnp.stack([upper_row, lower_row], axis=2)
    right_real = jnp.swapaxes(right_sel[:, :, 0], -1, -2)
    right_imag = jnp.swapaxes(right_sel[:, :, 1], -1, -2)
    first_col = jnp.stack([right_real, -right_imag], axis=3)
    second_col = jnp.stack([right_imag, right_real], axis=3)
    right_big = jnp.stack([first_col, second_col], axis=2)
    return left_big, right_big


def coupling(phonon_modes, phonon_weight, offset):
    span = jnp.arange(-E_DEV, E_DEV + 1, dtype=jnp.int32)
    chosen = (phonon_modes[:, 0] == offset).astype(jnp.float32)
    below = (span[None, :] == -phonon_modes[:, 1:2]).astype(jnp.float32)
    above = (span[None, :] == phonon_modes[:, 1:2]).astype(jnp.float32)
    terms = chosen[:, None, None] * (phonon_weight[:, :, 0:1] * below[:, None, :] + phonon_weight[:, :, 1:2] * above[:, None, :])
    return jnp.sum(terms, axis=0).astype(jnp.bfloat16)


def reference(green_tiles, dham_blocks, phonon_weight, phonon_modes, tile_pattern):
    left_big, right_big = stack_blocks(dham_blocks[:, tile_pattern[:, 0]], dham_blocks[:, tile_pattern[:, 1]])
    left_wide = left_big.astype(jnp.float32)
    right_wide = right_big.astype(jnp.float32)
    kernels = [coupling(phonon_modes, phonon_weight, offset).astype(jnp.float32) for offset in OFFSETS]

    def one_momentum(momentum):
        summed = jnp.zeros((NE, NT, 2, TS, TS), jnp.float32)
        for position, offset in enumerate(OFFSETS):
            source = ((momentum - offset) % NK).astype(jnp.int32)
            tiles = lax.dynamic_index_in_dim(green_tiles, source, 0, keepdims=False)
            padded = jnp.pad(tiles, ((E_DEV, E_DEV), (0, 0), (0, 0), (0, 0), (0, 0)))
            kern = kernels[position]
            accum = jnp.zeros((3, NE, NT, 2, TS, TS), jnp.float32)
            for column in range(2 * E_DEV + 1):
                segment = padded[column:column + NE].astype(jnp.float32)
                accum = accum + kern[:, column][:, None, None, None, None, None] * segment[None]
            mixed = accum.astype(jnp.bfloat16).astype(jnp.float32)
            product = jnp.einsum("dtbicj,detcjk->detbik", left_wide, mixed).astype(jnp.bfloat16)
            summed = summed + jnp.einsum("detcij,dtcjbk->etbik", product.astype(jnp.float32), right_wide)
        return summed.astype(jnp.bfloat16)

    return lax.map(one_momentum, jnp.arange(NK, dtype=jnp.int32))
```

```python
import functools
import jax
import jax.numpy as jnp
from jax import lax
from jax.experimental import pallas as pl
from jax.experimental.pallas import tpu as pltpu
from jax.sharding import PartitionSpec as P

AXES = ("energy", "momentum")
SLOTS = 3
DIRS = 3
ROWS = 32
GRANT = 16 * 2**20


def in_vmem(array):
    return pltpu.with_memory_space_constraint(array, pltpu.VMEM)


def vmem_specs(count):
    return [pl.BlockSpec(memory_space=pltpu.VMEM)] * count


def routes(n_e, n_k):
    def pairs(step):
        out = []
        for e in range(n_e):
            for k in range(n_k):
                to_e, to_k = step(e, k)
                if 0 <= to_e < n_e:
                    out.append((e * n_k + k, to_e * n_k + to_k % n_k))
        return out

    return {
        "pair": pairs(lambda e, k: (e ^ 1, k)),
        "relay": pairs(lambda e, k: (e + 2 - 4 * (e % 2), k)),
        "back": pairs(lambda e, k: (e - 2 + 4 * (e % 2), k)),
        "core": pairs(lambda e, k: (e, k ^ 1)),
        "far": pairs(lambda e, k: (e, k - 1 + 2 * (k % 2))),
    }


def prepare_kernel(parity, modes, weight, pattern, dham, left, right, coef_in, coef_out, table):
    mode_count = modes.shape[0]
    tile_count = pattern.shape[0]
    for q in range(4):
        for d in range(DIRS):
            for s in range(9):
                table[q, d, s] = 0.0
    for m in range(mode_count):
        q = modes[m, 0] + 1
        step = modes[m, 1]
        for d in range(DIRS):
            table[q, d, 4 - step] = table[q, d, 4 - step] + weight[m, d, 0]
            table[q, d, 4 + step] = table[q, d, 4 + step] + weight[m, d, 1]
    e_dir = 1 - 2 * parity[0]
    k_dir = 1 - 2 * parity[1]
    e_dirs = (0, e_dir, -e_dir)
    k_dirs = (0, k_dir, -k_dir)

    def spread(value):
        return jnp.full((8, 128), value, jnp.float32).astype(jnp.bfloat16).astype(jnp.float32)

    for d in range(DIRS):
        for slot in range(SLOTS):
            for i in range(2):
                for block in range(SLOTS):
                    for j in range(2):
                        entry = ((d * SLOTS + slot) * 2 + i) * 6 + block * 2 + j
                        shift = j - i + 2 * e_dirs[block]
                        coef_in[entry] = spread(table[k_dirs[slot] + 1, d, shift + 4])
                        shift = j - i - 2 * e_dirs[slot]
                        coef_out[entry] = spread(table[1 - k_dirs[block], d, shift + 4])
    for t in range(tile_count):
        lo, hi = pattern[t, 0], pattern[t, 1]
        for d in range(DIRS):
            real, imag = dham[d, lo, 0], dham[d, lo, 1]
            left[t, d, :128, :128] = real
            left[t, d, :128, 128:] = -imag
            left[t, d, 128:, :128] = imag
            left[t, d, 128:, 128:] = real
            real, imag = dham[d, hi, 0].T, dham[d, hi, 1].T
            right[t, d, :128, :128] = real
            right[t, d, :128, 128:] = -imag
            right[t, d, 128:, :128] = imag
            right[t, d, 128:, 128:] = real


def prepare(parity, modes, weight, pattern, dham):
    tile_count = pattern.shape[0]
    entries = DIRS * SLOTS * 2 * 6
    big = pltpu.VMEM((tile_count, DIRS, 256, 256), jnp.bfloat16)
    coef = pltpu.VMEM((entries, 8, 128), jnp.float32)
    return pl.pallas_call(
        prepare_kernel,
        out_shape=(big, big, coef, coef),
        in_specs=[pl.BlockSpec(memory_space=pltpu.SMEM)] * 4 + vmem_specs(1),
        out_specs=tuple(vmem_specs(4)),
        scratch_shapes=[pltpu.SMEM((4, DIRS, 9), jnp.float32)],
        compiler_params=pltpu.CompilerParams(vmem_limit_bytes=GRANT),
        name="prepare",
    )(parity, modes, weight, pattern, dham)


def sandwich_kernel(first, own, near, far, left, right, coef, to_own, to_near, to_far, mixed, product):
    tiles = own.shape[1]
    outs = (to_own, to_near, to_far)
    sources = (own, near, far)
    for t in range(tiles):
        for part in range(2):
            for row in range(0, 128, ROWS):
                taken = [
                    sources[block][j, t, part, pl.ds(row, ROWS), :].astype(jnp.float32).reshape(ROWS // 8, 8, 128)
                    for block in range(SLOTS)
                    for j in range(2)
                ]
                for d in range(DIRS):
                    for item in range(2 * SLOTS):
                        base = (d * 2 * SLOTS + item) * 6
                        acc = taken[0] * coef[base]
                        for tap in range(1, 6):
                            acc = acc + taken[tap] * coef[base + tap]
                        mixed[t, d, pl.ds(part * 128 + row, ROWS), pl.ds(item * 128, 128)] = acc.reshape(ROWS, 128).astype(jnp.bfloat16)
        for d in range(DIRS):
            got = jnp.dot(left[first + t, d], mixed[t, d], preferred_element_type=jnp.float32).astype(jnp.bfloat16)
            for item in range(2 * SLOTS):
                for part in range(2):
                    product[t, pl.ds(item * 128, 128), pl.ds(d * 256 + part * 128, 128)] = got[
                        part * 128 : part * 128 + 128, item * 128 : item * 128 + 128
                    ]
        weights = right[first + t].reshape(DIRS * 256, 256)
        term = jnp.dot(product[t], weights, preferred_element_type=jnp.float32)
        for slot in range(SLOTS):
            for i in range(2):
                item = slot * 2 + i
                for part in range(2):
                    outs[slot][i, t, part] = term[item * 128 : item * 128 + 128, part * 128 : part * 128 + 128].astype(outs[slot].dtype)


def sandwich(first, own, near, far, left, right, coef, near_type):
    shape = own.shape
    tiles = shape[1]
    return pl.pallas_call(
        functools.partial(sandwich_kernel, first),
        out_shape=(
            pltpu.VMEM(shape, jnp.float32),
            pltpu.VMEM(shape, near_type),
            pltpu.VMEM(shape, jnp.bfloat16),
        ),
        in_specs=vmem_specs(6),
        out_specs=tuple(vmem_specs(3)),
        scratch_shapes=[
            pltpu.VMEM((tiles, DIRS, 256, 2 * SLOTS * 128), jnp.bfloat16),
            pltpu.VMEM((tiles, 2 * SLOTS * 128, DIRS * 256), jnp.bfloat16),
        ],
        compiler_params=pltpu.CompilerParams(vmem_limit_bytes=GRANT),
        name="sandwich",
    )(in_vmem(own), in_vmem(near), in_vmem(far), in_vmem(left), in_vmem(right), in_vmem(coef))


def add_kernel(a, b, out):
    out[...] = (a[...] + b[...].astype(jnp.float32)).astype(out.dtype)


def add(a, b):
    return pl.pallas_call(
        add_kernel,
        out_shape=pltpu.VMEM(a.shape, jnp.bfloat16),
        in_specs=vmem_specs(2),
        out_specs=vmem_specs(1)[0],
        compiler_params=pltpu.CompilerParams(vmem_limit_bytes=GRANT),
        name="add",
    )(in_vmem(a), in_vmem(b))


def finish_kernel(own_a, near_a, far_a, own_b, near_b, out):
    tiles = own_a.shape[1]
    f32 = jnp.float32
    out[0, :, :tiles] = (own_a[...] + near_a[...].astype(f32) + far_a[...].astype(f32)).astype(out.dtype)
    out[0, :, tiles:] = (own_b[...] + near_b[...].astype(f32)).astype(out.dtype)


def finish(own_a, near_a, far_a, own_b, near_b):
    e, ta = own_a.shape[:2]
    shape = (1, e, ta + own_b.shape[1]) + own_a.shape[2:]
    return pl.pallas_call(
        finish_kernel,
        out_shape=jax.ShapeDtypeStruct(shape, jnp.bfloat16),
        in_specs=vmem_specs(5),
        out_specs=vmem_specs(1)[0],
        compiler_params=pltpu.CompilerParams(vmem_limit_bytes=GRANT),
        name="finish",
    )(*map(in_vmem, (own_a, near_a, far_a, own_b, near_b)))


def local(green_tiles, dham_blocks, phonon_weight, phonon_modes, tile_pattern):
    n_e, n_k = (lax.axis_size(axis) for axis in AXES)
    route = routes(n_e, n_k)

    def send(block, name):
        return lax.ppermute(block, AXES, route[name])

    tiles = green_tiles[0]
    half = tiles.shape[1] // 2
    in_a, in_b = tiles[:, :half], tiles[:, half:]
    parity = jnp.stack([lax.axis_index(axis) % 2 for axis in AXES]).astype(jnp.int32)
    near_a = send(in_a, "pair")
    far_b = send(in_b, "far")
    near_b = send(in_b, "core")
    left, right, coef_in, coef_out = prepare(parity, phonon_modes, phonon_weight, tile_pattern, dham_blocks)
    far_a = send(near_a, "relay")
    own_b, pair_b, cross_b = sandwich(half, in_b, near_b, far_b, left, right, coef_out, jnp.float32)
    cross_b = send(cross_b, "back")
    own_a, core_a, next_a = sandwich(0, in_a, near_a, far_a, left, right, coef_in, jnp.bfloat16)
    next_a = send(next_a, "far")
    core_a = send(core_a, "core")
    pair_b = send(add(pair_b, cross_b), "pair")
    return finish(own_a, core_a, next_a, own_b, pair_b)


def solution(mesh):
    placed = (P("momentum", "energy", None, None, None, None), P(), P(), P(), P())
    return jax.shard_map(
        local,
        mesh=mesh,
        in_specs=placed,
        out_specs=P("momentum", "energy", None, None, None, None),
        check_vma=False,
    )
```

```python
import functools
import jax
import jax.numpy as jnp
from jax import lax
from jax.experimental import pallas as pl
from jax.experimental.pallas import tpu as pltpu
from jax.sharding import PartitionSpec as P

AXES = ("energy", "momentum")
DIRS = 3
REACH = 2
EVEN = 3 * DIRS * (2 * REACH + 1)
AT_REST = EVEN + 1
ENTRIES = EVEN + 2
ROWS = 32
GRANT = 16 * 2**20


def in_vmem(array):
    return pltpu.with_memory_space_constraint(array, pltpu.VMEM)


def in_hbm(array):
    return pltpu.with_memory_space_constraint(array, pltpu.HBM)


def vmem_specs(count):
    return [pl.BlockSpec(memory_space=pltpu.VMEM)] * count


def routes(n_e, n_k):
    def pairs(step):
        out = []
        for e in range(n_e):
            for k in range(n_k):
                to_e, to_k = step(e, k)
                if 0 <= to_e < n_e:
                    out.append((e * n_k + k, to_e * n_k + to_k % n_k))
        return out

    return {
        "pair": pairs(lambda e, k: (e ^ 1, k)),
        "relay": pairs(lambda e, k: (e + 2 - 4 * (e % 2), k)),
        "cross": pairs(lambda e, k: (e - 1 + 2 * (e % 2), k)),
        "core": pairs(lambda e, k: (e, k ^ 1)),
        "far": pairs(lambda e, k: (e, k - 1 + 2 * (k % 2))),
    }


def prepare_kernel(parity, modes, weight, pattern, dham, left, right, coef, table):
    mode_count = modes.shape[1]
    tile_count = pattern.shape[1]
    for q in range(4):
        for d in range(DIRS):
            for s in range(2 * REACH + 1):
                table[q, d, s] = 0.0
    for m in range(mode_count):
        q = modes[0, m] + 1
        step = modes[1, m]
        for d in range(DIRS):
            table[q, d, REACH - step] = table[q, d, REACH - step] + weight[d, 0, m]
            table[q, d, REACH + step] = table[q, d, REACH + step] + weight[d, 1, m]
    toward = 1 - 2 * parity[1]
    at_rest = 0.0
    for slot, q in enumerate((0, toward, -toward)):
        for d in range(DIRS):
            for s in range(2 * REACH + 1):
                value = table[q + 1, d, s]
                if s == REACH:
                    at_rest = at_rest + jnp.abs(value)
                value = jnp.full((8, 128), value, jnp.float32)
                coef[(slot * DIRS + d) * (2 * REACH + 1) + s] = value.astype(jnp.bfloat16).astype(jnp.float32)
    coef[EVEN] = jnp.full((8, 128), 1 - parity[0], jnp.int32).astype(jnp.float32)
    coef[AT_REST] = jnp.full((8, 128), at_rest, jnp.float32)
    for t in range(tile_count):
        lo, hi = pattern[0, t], pattern[1, t]
        for d in range(DIRS):
            real, imag = dham[d, lo, 0], dham[d, lo, 1]
            left[t, d, :128, :128] = real
            left[t, d, :128, 128:] = -imag
            left[t, d, 128:, :128] = imag
            left[t, d, 128:, 128:] = real
            real, imag = dham[d, hi, 0].T, dham[d, hi, 1].T
            right[t, d, :128, :128] = real
            right[t, d, :128, 128:] = -imag
            right[t, d, 128:, :128] = imag
            right[t, d, 128:, 128:] = real


def prepare(parity, modes, weight, pattern, dham):
    tile_count = pattern.shape[1]
    big = pltpu.VMEM((tile_count, DIRS, 256, 256), jnp.bfloat16)
    return pl.pallas_call(
        prepare_kernel,
        out_shape=(big, big, pltpu.VMEM((ENTRIES, 8, 128), jnp.float32)),
        in_specs=[pl.BlockSpec(memory_space=pltpu.SMEM)] * 4 + vmem_specs(1),
        out_specs=tuple(vmem_specs(3)),
        scratch_shapes=[pltpu.SMEM((4, DIRS, 2 * REACH + 1), jnp.float32)],
        compiler_params=pltpu.CompilerParams(vmem_limit_bytes=GRANT),
        name="prepare",
    )(parity, in_hbm(modes), in_hbm(weight), in_hbm(pattern), in_hbm(dham))


def mix(t, forward, steps, sources, coef, mixed):
    even = coef[EVEN] > 0.5
    own, near, far = sources

    def at(slot, d, s):
        return coef[(slot * DIRS + d) * (2 * REACH + 1) + s + REACH]

    for part in range(2):
        for row in range(0, 128, ROWS):

            def load(ref, j):
                return ref[j, t, part, pl.ds(row, ROWS), :].astype(jnp.float32).reshape(ROWS // 8, 8, 128)

            taken = [[load(ref, j) for j in range(2)] for ref in sources]
            if forward:
                below = [jnp.where(even, b, a) for a, b in zip(taken[1], taken[2])]
                above = [jnp.where(even, a, b) for a, b in zip(taken[1], taken[2])]
                line = below + taken[0] + above
            for d in range(DIRS):
                for item in range(6):
                    if forward:
                        slot, i = divmod(item, 2)
                        terms = [(line[2 + i + s], at(slot, d, s)) for s in steps]
                    else:
                        place = item - 2
                        terms = [(taken[m][j], at((0, 2, 1)[m], d, j - place)) for m in range(3) for j in range(2) if j - place in steps]
                    acc = terms[0][0] * terms[0][1]
                    for value, factor in terms[1:]:
                        acc = acc + value * factor
                    mixed[t, d, pl.ds(part * 128 + row, ROWS), pl.ds(item * 128, 128)] = acc.reshape(ROWS, 128).astype(jnp.bfloat16)


def multiply(t, first, forward, left, right, coef, outs, mixed, product):
    for d in range(DIRS):
        got = jnp.dot(left[first + t, d], mixed[t, d], preferred_element_type=jnp.float32).astype(jnp.bfloat16)
        for item in range(6):
            for part in range(2):
                product[t, pl.ds(item * 128, 128), pl.ds(d * 256 + part * 128, 128)] = got[
                    part * 128 : part * 128 + 128, item * 128 : item * 128 + 128
                ]
    term = jnp.dot(product[t], right[first + t].reshape(DIRS * 256, 256), preferred_element_type=jnp.float32)
    even = jnp.broadcast_to(coef[EVEN][:1] > 0.5, (128, 128))
    for i in range(2):
        for part in range(2):

            def result(item):
                return term[item * 128 : item * 128 + 128, part * 128 : part * 128 + 128]

            if forward:
                values = [result(slot * 2 + i) for slot in range(3)]
            else:
                below, own, above = (result(block * 2 + i) for block in range(3))
                values = [own, jnp.where(even, above, below), jnp.where(even, below, above)]
            for out, value in zip(outs, values):
                out[i, t, part] = value.astype(out.dtype)


def sandwich_kernel(first, forward, own, near, far, left, right, coef, to_own, to_near, to_far, mixed, product):
    tiles = own.shape[1]
    outs = (to_own, to_near, to_far)
    at_rest = jnp.max(coef[AT_REST])

    def run(t, steps):
        mix(t, forward, steps, (own, near, far), coef, mixed)
        multiply(t, first, forward, left, right, coef, outs, mixed, product)

    @pl.when(at_rest == 0.0)
    def _():
        for t in range(tiles):
            run(t, (-2, -1, 1, 2))

    @pl.when(at_rest != 0.0)
    def _():
        @pl.loop(0, tiles)
        def _(t):
            run(t, (-2, -1, 0, 1, 2))


def sandwich(first, forward, own, near, far, left, right, coef):
    shape = own.shape
    tiles = shape[1]
    return pl.pallas_call(
        functools.partial(sandwich_kernel, first, forward),
        out_shape=(
            pltpu.VMEM(shape, jnp.float32),
            pltpu.VMEM(shape, jnp.bfloat16),
            pltpu.VMEM(shape, jnp.bfloat16),
        ),
        in_specs=vmem_specs(6),
        out_specs=tuple(vmem_specs(3)),
        scratch_shapes=[
            pltpu.VMEM((tiles, DIRS, 256, 6 * 128), jnp.bfloat16),
            pltpu.VMEM((tiles, 6 * 128, DIRS * 256), jnp.bfloat16),
        ],
        compiler_params=pltpu.CompilerParams(vmem_limit_bytes=GRANT),
        cost_estimate=pl.CostEstimate(flops=1_200_000_000 * tiles, bytes_accessed=4_000_000 * tiles, transcendentals=0),
        name="sandwich",
    )(in_vmem(own), in_vmem(near), in_vmem(far), in_vmem(left), in_vmem(right), in_vmem(coef))


def gather_kernel(own, near, far, out):
    f32 = jnp.float32
    out[...] = (own[...] + near[...].astype(f32) + far[...].astype(f32)).astype(out.dtype)


def gather(own, near, far):
    return pl.pallas_call(
        gather_kernel,
        out_shape=pltpu.VMEM(own.shape, jnp.bfloat16),
        in_specs=vmem_specs(3),
        out_specs=vmem_specs(1)[0],
        compiler_params=pltpu.CompilerParams(vmem_limit_bytes=GRANT),
        cost_estimate=pl.CostEstimate(flops=4_000_000_000, bytes_accessed=16_000_000, transcendentals=0),
        name="gather",
    )(*map(in_vmem, (own, near, far)))


def finish_kernel(own_a, near_a, far_a, done_b, out, held, sems):
    tiles_a, tiles_b = own_a.shape[1], done_b.shape[1]
    f32 = jnp.float32
    copies = [pltpu.make_async_copy(done_b, out.at[0, :, pl.ds(tiles_a, tiles_b)], sems.at[tiles_a])]
    copies[0].start()
    for t in range(tiles_a):
        held[:, t] = (own_a[:, t] + near_a[:, t].astype(f32) + far_a[:, t].astype(f32)).astype(held.dtype)
        copies.append(pltpu.make_async_copy(held.at[:, t], out.at[0, :, t], sems.at[t]))
        copies[-1].start()
    for copy in copies:
        copy.wait()


def finish(own_a, near_a, far_a, done_b):
    e, tiles_a = own_a.shape[:2]
    rest = own_a.shape[2:]
    return pl.pallas_call(
        finish_kernel,
        out_shape=jax.ShapeDtypeStruct((1, e, tiles_a + done_b.shape[1]) + rest, jnp.bfloat16),
        in_specs=vmem_specs(4),
        out_specs=pl.BlockSpec(memory_space=pl.ANY),
        scratch_shapes=[pltpu.VMEM((e, tiles_a) + rest, jnp.bfloat16), pltpu.SemaphoreType.DMA((tiles_a + 1,))],
        compiler_params=pltpu.CompilerParams(vmem_limit_bytes=GRANT),
        name="finish",
    )(*map(in_vmem, (own_a, near_a, far_a, done_b)))


def local(green_tiles, dham_blocks, phonon_weight, phonon_modes, tile_pattern):
    n_e, n_k = (lax.axis_size(axis) for axis in AXES)
    route = routes(n_e, n_k)

    def send(block, name):
        return lax.ppermute(block, AXES, route[name])

    tiles = green_tiles[0]
    half = tiles.shape[1] // 2
    in_a, in_b = tiles[:, :half], tiles[:, half:]
    parity = jnp.stack([lax.axis_index(axis) % 2 for axis in AXES]).astype(jnp.int32)
    near_a = send(in_a, "pair")
    far_b = send(in_b, "far")
    near_b = send(in_b, "core")
    left, right, coef = prepare(parity, phonon_modes.T, phonon_weight.transpose(1, 2, 0), tile_pattern.T, dham_blocks)
    near_a, left = lax.optimization_barrier((near_a, left))
    far_a = send(near_a, "relay")
    far_b, near_a = lax.optimization_barrier((far_b, near_a))
    own_b, pair_b, cross_b = sandwich(half, False, in_b, near_b, far_b, left, right, coef)
    pair_b = send(pair_b, "pair")
    cross_b = send(cross_b, "cross")
    own_a, core_a, next_a = sandwich(0, True, in_a, near_a, far_a, left, right, coef)
    next_a = send(next_a, "far")
    core_a = send(core_a, "core")
    done_b = gather(own_b, pair_b, cross_b)
    return finish(own_a, core_a, next_a, done_b)


def solution(mesh):
    placed = (P("momentum", "energy", None, None, None, None), P(), P(), P(), P())
    return jax.shard_map(
        local,
        mesh=mesh,
        in_specs=placed,
        out_specs=P("momentum", "energy", None, None, None, None),
        check_vma=False,
    )
```

```python
import functools
import jax
import jax.numpy as jnp
from jax import lax
from jax.experimental import pallas as pl
from jax.experimental.pallas import tpu as pltpu
from jax.sharding import PartitionSpec as P

AXES = ("energy", "momentum")
DIRS = 3
REACH = 2
EVEN = 3 * DIRS * (2 * REACH + 1)
AT_REST = EVEN + 1
ENTRIES = EVEN + 2
ROWS = 32
GRANT = 16 * 2**20


def in_vmem(array):
    return pltpu.with_memory_space_constraint(array, pltpu.VMEM)


def in_hbm(array):
    return pltpu.with_memory_space_constraint(array, pltpu.HBM)


def vmem_specs(count):
    return [pl.BlockSpec(memory_space=pltpu.VMEM)] * count


def routes(n_e, n_k):
    def pairs(step):
        out = []
        for e in range(n_e):
            for k in range(n_k):
                to_e, to_k = step(e, k)
                if 0 <= to_e < n_e:
                    out.append((e * n_k + k, to_e * n_k + to_k % n_k))
        return out

    return {
        "pair": pairs(lambda e, k: (e ^ 1, k)),
        "relay": pairs(lambda e, k: (e + 2 - 4 * (e % 2), k)),
        "cross": pairs(lambda e, k: (e - 1 + 2 * (e % 2), k)),
        "core": pairs(lambda e, k: (e, k ^ 1)),
        "far": pairs(lambda e, k: (e, k - 1 + 2 * (k % 2))),
    }


def prepare_kernel(parity, modes, weight, pattern, dham, left, right, coef, table):
    mode_count = modes.shape[1]
    tile_count = pattern.shape[1]
    for q in range(4):
        for d in range(DIRS):
            for s in range(2 * REACH + 1):
                table[q, d, s] = 0.0
    for m in range(mode_count):
        q = modes[0, m] + 1
        step = modes[1, m]
        for d in range(DIRS):
            table[q, d, REACH - step] = table[q, d, REACH - step] + weight[d, 0, m]
            table[q, d, REACH + step] = table[q, d, REACH + step] + weight[d, 1, m]
    toward = 1 - 2 * parity[1]
    at_rest = 0.0
    for slot, q in enumerate((0, toward, -toward)):
        for d in range(DIRS):
            for s in range(2 * REACH + 1):
                value = table[q + 1, d, s]
                if s == REACH:
                    at_rest = at_rest + jnp.abs(value)
                value = jnp.full((8, 128), value, jnp.float32)
                coef[(slot * DIRS + d) * (2 * REACH + 1) + s] = value.astype(jnp.bfloat16).astype(jnp.float32)
    coef[EVEN] = jnp.full((8, 128), 1 - parity[0], jnp.int32).astype(jnp.float32)
    coef[AT_REST] = jnp.full((8, 128), at_rest, jnp.float32)
    for t in range(tile_count):
        lo, hi = pattern[0, t], pattern[1, t]
        for d in range(DIRS):
            real, imag = dham[d, lo, 0], dham[d, lo, 1]
            left[t, d, :128, :128] = real
            left[t, d, :128, 128:] = -imag
            left[t, d, 128:, :128] = imag
            left[t, d, 128:, 128:] = real
            real, imag = dham[d, hi, 0].T, dham[d, hi, 1].T
            right[t, d, :128, :128] = real
            right[t, d, :128, 128:] = -imag
            right[t, d, 128:, :128] = imag
            right[t, d, 128:, 128:] = real


def prepare(parity, modes, weight, pattern, dham):
    tile_count = pattern.shape[1]
    big = pltpu.VMEM((tile_count, DIRS, 256, 256), jnp.bfloat16)
    return pl.pallas_call(
        prepare_kernel,
        out_shape=(big, big, pltpu.VMEM((ENTRIES, 8, 128), jnp.float32)),
        in_specs=[pl.BlockSpec(memory_space=pltpu.SMEM)] * 4 + vmem_specs(1),
        out_specs=tuple(vmem_specs(3)),
        scratch_shapes=[pltpu.SMEM((4, DIRS, 2 * REACH + 1), jnp.float32)],
        compiler_params=pltpu.CompilerParams(vmem_limit_bytes=GRANT),
        name="prepare",
    )(parity, in_hbm(modes), in_hbm(weight), in_hbm(pattern), in_hbm(dham))


def mix(t, forward, steps, blocks, items, sources, coef, partial, out):
    even = coef[EVEN] > 0.5

    def at(slot, d, s):
        return coef[(slot * DIRS + d) * (2 * REACH + 1) + s + REACH]

    for part in range(2):
        for row in range(0, 128, ROWS):

            def load(ref, j):
                return ref[j, t, part, pl.ds(row, ROWS), :].astype(jnp.float32).reshape(ROWS // 8, 8, 128)

            taken = {block: [load(sources[block], j) for j in range(2)] for block in blocks}
            if forward:
                below = [jnp.where(even, b, a) for a, b in zip(taken[1], taken[2])]
                above = [jnp.where(even, a, b) for a, b in zip(taken[1], taken[2])]
                line = below + taken[0] + above
            for d in range(DIRS):
                for at_item, item in enumerate(items):
                    if forward:
                        slot, i = divmod(item, 2)
                        terms = [(line[2 + i + s], at(slot, d, s)) for s in steps]
                    else:
                        place = item - 2
                        terms = [(taken[m][j], at((0, 2, 1)[m], d, j - place)) for m in blocks for j in range(2) if j - place in steps]
                    here = (t, d, pl.ds(part * 128 + row, ROWS), pl.ds(at_item * 128, 128))
                    acc = terms[0][0] * terms[0][1]
                    if partial is not None:
                        acc = acc + partial[here].reshape(ROWS // 8, 8, 128)
                    for value, factor in terms[1:]:
                        acc = acc + value * factor
                    out[here] = acc.reshape(ROWS, 128).astype(out.dtype)


def multiply(t, first, count, left, right, mixed, product):
    for d in range(DIRS):
        got = jnp.dot(left[first + t, d], mixed[t, d], preferred_element_type=jnp.float32).astype(jnp.bfloat16)
        for item in range(count):
            for part in range(2):
                product[t, pl.ds(item * 128, 128), pl.ds(d * 256 + part * 128, 128)] = got[
                    part * 128 : part * 128 + 128, item * 128 : item * 128 + 128
                ]
    return jnp.dot(product[t], right[first + t].reshape(DIRS * 256, 256), preferred_element_type=jnp.float32)


def both_ways(coef, tiles, run):
    at_rest = jnp.max(coef[AT_REST])

    @pl.when(at_rest == 0.0)
    def _():
        for t in range(tiles):
            run(t, (-2, -1, 1, 2))

    @pl.when(at_rest != 0.0)
    def _():
        @pl.loop(0, tiles)
        def _(t):
            run(t, (-2, -1, 0, 1, 2))


def scratch(tiles, count):
    return [
        pltpu.VMEM((tiles, DIRS, 256, count * 128), jnp.bfloat16),
        pltpu.VMEM((tiles, count * 128, DIRS * 256), jnp.bfloat16),
    ]


SENT_IN, SENT_OUT, KEPT_IN, KEPT_OUT = (2, 3, 4, 5), (0, 1, 4, 5), (0, 1), (2, 3)


def premix_kernel(own, coef, partial):
    both_ways(coef, own.shape[1], lambda t, steps: mix(t, False, steps, (0,), SENT_OUT, (own,), coef, None, partial))


def premix(own, coef):
    tiles = own.shape[1]
    return pl.pallas_call(
        premix_kernel,
        out_shape=pltpu.VMEM((tiles, DIRS, 256, len(SENT_OUT) * 128), jnp.float32),
        in_specs=vmem_specs(2),
        out_specs=vmem_specs(1)[0],
        compiler_params=pltpu.CompilerParams(vmem_limit_bytes=GRANT),
        cost_estimate=pl.CostEstimate(flops=300_000_000 * tiles, bytes_accessed=1_000_000 * tiles, transcendentals=0),
        name="premix",
    )(in_vmem(own), in_vmem(coef))


def sent_kernel(first, forward, *refs):
    sources, (left, right, coef, to_near, to_far, mixed, product) = refs[:3], refs[3:]

    def run(t, steps):
        if forward:
            mix(t, True, steps, (0, 1, 2), SENT_IN, sources, coef, None, mixed)
        else:
            mix(t, False, steps, (1, 2), SENT_OUT, {1: sources[0], 2: sources[1]}, coef, sources[2], mixed)
        term = multiply(t, first, 4, left, right, mixed, product)
        even = jnp.broadcast_to(coef[EVEN][:1] > 0.5, (128, 128))
        for i in range(2):
            for part in range(2):
                one, two = (term[at * 128 : at * 128 + 128, part * 128 : part * 128 + 128] for at in (i, 2 + i))
                if not forward:
                    one, two = jnp.where(even, two, one), jnp.where(even, one, two)
                to_near[i, t, part] = one.astype(to_near.dtype)
                to_far[i, t, part] = two.astype(to_far.dtype)

    both_ways(coef, to_near.shape[1], run)


def sent(first, forward, sources, left, right, coef):
    shape = sources[0].shape
    tiles = shape[1]
    operands = (*sources, left, right, coef)
    return pl.pallas_call(
        functools.partial(sent_kernel, first, forward),
        out_shape=(pltpu.VMEM(shape, jnp.bfloat16), pltpu.VMEM(shape, jnp.bfloat16)),
        in_specs=vmem_specs(len(operands)),
        out_specs=tuple(vmem_specs(2)),
        scratch_shapes=scratch(tiles, 4),
        compiler_params=pltpu.CompilerParams(vmem_limit_bytes=GRANT),
        cost_estimate=pl.CostEstimate(flops=1_200_000_000 * tiles, bytes_accessed=4_000_000 * tiles, transcendentals=0),
        name="sent",
    )(*map(in_vmem, operands))


def kept_kernel(*refs):
    sources_a, sources_b, (left, right, coef, own_a, own_b, mixed_a, product_a, mixed_b, product_b) = refs[:3], refs[3:6], refs[6:]
    half = own_a.shape[1]

    def run(first, forward, items, sources, out, mixed, product, t, steps):
        mix(t, forward, steps, (0, 1, 2), items, sources, coef, None, mixed)
        term = multiply(t, first, 2, left, right, mixed, product)
        for i in range(2):
            for part in range(2):
                out[i, t, part] = term[i * 128 : i * 128 + 128, part * 128 : part * 128 + 128]

    both_ways(coef, half, functools.partial(run, 0, True, KEPT_IN, sources_a, own_a, mixed_a, product_a))
    both_ways(coef, own_b.shape[1], functools.partial(run, half, False, KEPT_OUT, sources_b, own_b, mixed_b, product_b))


def kept(sources_a, sources_b, left, right, coef):
    shape_a, shape_b = sources_a[0].shape, sources_b[0].shape
    operands = (*sources_a, *sources_b, left, right, coef)
    return pl.pallas_call(
        kept_kernel,
        out_shape=(pltpu.VMEM(shape_a, jnp.float32), pltpu.VMEM(shape_b, jnp.float32)),
        in_specs=vmem_specs(len(operands)),
        out_specs=tuple(vmem_specs(2)),
        scratch_shapes=scratch(shape_a[1], 2) + scratch(shape_b[1], 2),
        compiler_params=pltpu.CompilerParams(vmem_limit_bytes=GRANT),
        cost_estimate=pl.CostEstimate(flops=2_400_000_000, bytes_accessed=8_000_000, transcendentals=0),
        name="kept",
    )(*map(in_vmem, operands))


def gather_kernel(near, far, out):
    out[...] = near[...].astype(jnp.float32) + far[...].astype(jnp.float32)


def gather(near, far):
    return pl.pallas_call(
        gather_kernel,
        out_shape=pltpu.VMEM(near.shape, jnp.float32),
        in_specs=vmem_specs(2),
        out_specs=vmem_specs(1)[0],
        compiler_params=pltpu.CompilerParams(vmem_limit_bytes=GRANT),
        cost_estimate=pl.CostEstimate(flops=1000_000_000, bytes_accessed=1000_000, transcendentals=0),
        name="gather",
    )(in_vmem(near), in_vmem(far))


def finish_kernel(own_a, near_a, far_a, own_b, from_b, out, held, sems):
    tiles_a, tiles_b = own_a.shape[1], own_b.shape[1]
    f32 = jnp.float32
    copies = []
    for t in range(tiles_a + tiles_b):
        if t < tiles_a:
            value = own_a[:, t] + near_a[:, t].astype(f32) + far_a[:, t].astype(f32)
        else:
            value = own_b[:, t - tiles_a] + from_b[:, t - tiles_a]
        held[:, t] = value.astype(held.dtype)
        copies.append(pltpu.make_async_copy(held.at[:, t], out.at[0, :, t], sems.at[t]))
        copies[-1].start()
    for copy in copies:
        copy.wait()


def finish(own_a, near_a, far_a, own_b, from_b):
    e, tiles_a = own_a.shape[:2]
    tiles = tiles_a + own_b.shape[1]
    shape = (e, tiles) + own_a.shape[2:]
    return pl.pallas_call(
        finish_kernel,
        out_shape=jax.ShapeDtypeStruct((1,) + shape, jnp.bfloat16),
        in_specs=vmem_specs(5),
        out_specs=pl.BlockSpec(memory_space=pl.ANY),
        scratch_shapes=[pltpu.VMEM(shape, jnp.bfloat16), pltpu.SemaphoreType.DMA((tiles,))],
        compiler_params=pltpu.CompilerParams(vmem_limit_bytes=GRANT),
        name="finish",
    )(*map(in_vmem, (own_a, near_a, far_a, own_b, from_b)))


def local(green_tiles, dham_blocks, phonon_weight, phonon_modes, tile_pattern):
    n_e, n_k = (lax.axis_size(axis) for axis in AXES)
    route = routes(n_e, n_k)

    def send(block, name):
        return lax.ppermute(block, AXES, route[name])

    tiles = green_tiles[0]
    half = tiles.shape[1] // 2
    in_a, in_b = tiles[:, :half], tiles[:, half:]
    parity = jnp.stack([lax.axis_index(axis) % 2 for axis in AXES]).astype(jnp.int32)
    near_a = send(in_a, "pair")
    far_b = send(in_b, "far")
    near_b = send(in_b, "core")
    left, right, coef = prepare(parity, phonon_modes.T, phonon_weight.transpose(1, 2, 0), tile_pattern.T, dham_blocks)
    partial_b = premix(in_b, coef)
    near_a, partial_b = lax.optimization_barrier((near_a, partial_b))
    far_a = send(near_a, "relay")
    far_b, near_a = lax.optimization_barrier((far_b, near_a))
    pair_b, cross_b = sent(half, False, (near_b, far_b, partial_b), left, right, coef)
    pair_b = send(pair_b, "pair")
    cross_b = send(cross_b, "cross")
    core_a, next_a = sent(0, True, (in_a, near_a, far_a), left, right, coef)
    in_b, next_a = lax.optimization_barrier((in_b, next_a))
    core_a = send(core_a, "core")
    next_a = send(next_a, "far")
    own_a, own_b = kept((in_a, near_a, far_a), (in_b, near_b, far_b), left, right, coef)
    own_b, pair_b = lax.optimization_barrier((own_b, pair_b))
    return finish(own_a, core_a, next_a, own_b, gather(pair_b, cross_b))


def solution(mesh):
    placed = (P("momentum", "energy", None, None, None, None), P(), P(), P(), P())
    return jax.shard_map(
        local,
        mesh=mesh,
        in_specs=placed,
        out_specs=P("momentum", "energy", None, None, None, None),
        check_vma=False,
    )
```

```python
import functools
import itertools
import jax
import jax.numpy as jnp
from jax import lax
from jax.experimental import pallas as pl
from jax.experimental.pallas import tpu as pltpu
from jax.sharding import PartitionSpec as P

AXES = ("energy", "momentum")
DIRS = 3
REACH = 2
EVEN = 3 * DIRS * (2 * REACH + 1)
AT_REST = EVEN + 1
INNER = EVEN + 2
ENTRIES = EVEN + 3
ROWS = 32
GRANT = 16 * 2**20


def in_vmem(array):
    return pltpu.with_memory_space_constraint(array, pltpu.VMEM)


def in_hbm(array):
    return pltpu.with_memory_space_constraint(array, pltpu.HBM)


def vmem_specs(count):
    return [pl.BlockSpec(memory_space=pltpu.VMEM)] * count


def routes(n_e, n_k):
    def pairs(step):
        return [(e * n_k + k, to_e * n_k + to_k % n_k) for e in range(n_e) for k in range(n_k) for to_e, to_k in [step(e, k)]]

    def inside(e, otherwise):
        return e if 0 <= e < n_e else otherwise

    return {
        "pair": pairs(lambda e, k: (e ^ 1, k)),
        "relay": pairs(lambda e, k: (inside(e + 2 - 4 * (e % 2), e ^ 1), k)),
        "cross": pairs(lambda e, k: (inside(e - 1 + 2 * (e % 2), e), k ^ (0 <= e - 1 + 2 * (e % 2) < n_e) ^ 1)),
        "core": pairs(lambda e, k: (e, k ^ 1)),
        "far": pairs(lambda e, k: (e, k - 1 + 2 * (k % 2))),
    }


def prepare_kernel(parity, modes, weight, pattern, dham, left, right, coef, table):
    mode_count = modes.shape[1]
    tile_count = pattern.shape[1]
    for q in range(4):
        for d in range(DIRS):
            for s in range(2 * REACH + 1):
                table[q, d, s] = 0.0
    for m in range(mode_count):
        q = modes[0, m] + 1
        step = modes[1, m]
        for d in range(DIRS):
            table[q, d, REACH - step] = table[q, d, REACH - step] + weight[d, 0, m]
            table[q, d, REACH + step] = table[q, d, REACH + step] + weight[d, 1, m]
    toward = 1 - 2 * parity[1]
    at_rest = 0.0
    for slot, q in enumerate((0, toward, -toward)):
        for d in range(DIRS):
            for s in range(2 * REACH + 1):
                value = table[q + 1, d, s]
                if s == REACH:
                    at_rest = at_rest + jnp.abs(value)
                value = jnp.full((8, 128), value, jnp.float32)
                coef[(slot * DIRS + d) * (2 * REACH + 1) + s] = value.astype(jnp.bfloat16).astype(jnp.float32)
    coef[EVEN] = jnp.full((8, 128), 1 - parity[0], jnp.int32).astype(jnp.float32)
    coef[INNER] = jnp.full((8, 128), parity[2], jnp.int32).astype(jnp.float32)
    coef[AT_REST] = jnp.full((8, 128), at_rest, jnp.float32)
    for t in range(tile_count):
        lo, hi = pattern[0, t], pattern[1, t]
        for d in range(DIRS):
            real, imag = dham[d, lo, 0], dham[d, lo, 1]
            left[t, d, :128, :128] = real
            left[t, d, :128, 128:] = -imag
            left[t, d, 128:, :128] = imag
            left[t, d, 128:, 128:] = real
            real, imag = dham[d, hi, 0].T, dham[d, hi, 1].T
            right[t, d, :128, :128] = real
            right[t, d, :128, 128:] = -imag
            right[t, d, 128:, :128] = imag
            right[t, d, 128:, 128:] = real


def prepare(parity, modes, weight, pattern, dham):
    tile_count = pattern.shape[1]
    big = pltpu.VMEM((tile_count, DIRS, 256, 256), jnp.bfloat16)
    return pl.pallas_call(
        prepare_kernel,
        out_shape=(big, big, pltpu.VMEM((ENTRIES, 8, 128), jnp.float32)),
        in_specs=[pl.BlockSpec(memory_space=pltpu.SMEM)] * 4 + vmem_specs(1),
        out_specs=tuple(vmem_specs(3)),
        scratch_shapes=[pltpu.SMEM((4, DIRS, 2 * REACH + 1), jnp.float32)],
        compiler_params=pltpu.CompilerParams(vmem_limit_bytes=GRANT),
        name="prepare",
    )(parity, in_hbm(modes), in_hbm(weight), in_hbm(pattern), in_hbm(dham))


def mix(t, forward, steps, blocks, items, sources, coef, partial, out):
    even, inner = coef[EVEN] > 0.5, coef[INNER] > 0.5

    def at(slot, d, s):
        return coef[(slot * DIRS + d) * (2 * REACH + 1) + s + REACH]

    for part in range(2):
        for row in range(0, 128, ROWS):

            def load(ref, j):
                return ref[j, t, part, pl.ds(row, ROWS), :].astype(jnp.float32).reshape(ROWS // 8, 8, 128)

            taken = {block: [load(sources[block], j) for j in range(2)] for block in blocks}
            if forward:
                taken[2] = [jnp.where(inner, value, 0.0) for value in taken[2]]
                below = [jnp.where(even, b, a) for a, b in zip(taken[1], taken[2])]
                above = [jnp.where(even, a, b) for a, b in zip(taken[1], taken[2])]
                line = below + taken[0] + above
            for d in range(DIRS):
                for at_item, item in enumerate(items):
                    if forward:
                        slot, i = divmod(item, 2)
                        terms = [(line[2 + i + s], at(slot, d, s)) for s in steps]
                    else:
                        place = item - 2
                        terms = [(taken[m][j], at((0, 2, 1)[m], d, j - place)) for m in blocks for j in range(2) if j - place in steps]
                    here = (t, d, pl.ds(part * 128 + row, ROWS), pl.ds(at_item * 128, 128))
                    acc = terms[0][0] * terms[0][1]
                    if partial is not None:
                        acc = acc + partial[here].reshape(ROWS // 8, 8, 128)
                    for value, factor in terms[1:]:
                        acc = acc + value * factor
                    out[here] = acc.reshape(ROWS, 128).astype(out.dtype)


def multiply(t, first, count, left, right, mixed, product):
    for d in range(DIRS):
        got = jnp.dot(left[first + t, d], mixed[t, d], preferred_element_type=jnp.float32).astype(jnp.bfloat16)
        for item in range(count):
            for part in range(2):
                product[t, pl.ds(item * 128, 128), pl.ds(d * 256 + part * 128, 128)] = got[
                    part * 128 : part * 128 + 128, item * 128 : item * 128 + 128
                ]
    return jnp.dot(product[t], right[first + t].reshape(DIRS * 256, 256), preferred_element_type=jnp.float32)


def both_ways(coef, tiles, run):
    at_rest = jnp.max(coef[AT_REST])

    @pl.when(at_rest == 0.0)
    def _():
        for t in range(tiles):
            run(t, (-2, -1, 1, 2))

    @pl.when(at_rest != 0.0)
    def _():
        @pl.loop(0, tiles)
        def _(t):
            run(t, (-2, -1, 0, 1, 2))


def scratch(tiles, count):
    return [
        pltpu.VMEM((tiles, DIRS, 256, count * 128), jnp.bfloat16),
        pltpu.VMEM((tiles, count * 128, DIRS * 256), jnp.bfloat16),
    ]


SENT_IN, SENT_OUT, KEPT_IN, KEPT_OUT = (2, 3, 4, 5), (0, 1, 4, 5), (0, 1), (2, 3)


def premix_kernel(own, coef, partial):
    both_ways(coef, own.shape[1], lambda t, steps: mix(t, False, steps, (0,), SENT_OUT, (own,), coef, None, partial))


def premix(own, coef):
    tiles = own.shape[1]
    return pl.pallas_call(
        premix_kernel,
        out_shape=pltpu.VMEM((tiles, DIRS, 256, len(SENT_OUT) * 128), jnp.float32),
        in_specs=vmem_specs(2),
        out_specs=vmem_specs(1)[0],
        compiler_params=pltpu.CompilerParams(vmem_limit_bytes=GRANT),
        cost_estimate=pl.CostEstimate(flops=300_000_000 * tiles, bytes_accessed=1_000_000 * tiles, transcendentals=0),
        name="premix",
    )(in_vmem(own), in_vmem(coef))


def sent_kernel(first, forward, *refs):
    sources, (left, right, coef, to_near, to_far, mixed, product) = refs[:3], refs[3:]

    def run(t, steps):
        if forward:
            mix(t, True, steps, (0, 1, 2), SENT_IN, sources, coef, None, mixed)
        else:
            mix(t, False, steps, (1, 2), SENT_OUT, {1: sources[0], 2: sources[1]}, coef, sources[2], mixed)
        term = multiply(t, first, 4, left, right, mixed, product)
        even = jnp.broadcast_to(coef[EVEN][:1] > 0.5, (128, 128))
        for i in range(2):
            for part in range(2):
                one, two = (term[at * 128 : at * 128 + 128, part * 128 : part * 128 + 128] for at in (i, 2 + i))
                if not forward:
                    one, two = jnp.where(even, two, one), jnp.where(even, one, two)
                to_near[i, t, part] = one.astype(to_near.dtype)
                to_far[i, t, part] = two.astype(to_far.dtype)

    both_ways(coef, to_near.shape[1], run)


def sent(first, forward, sources, left, right, coef):
    shape = sources[0].shape
    tiles = shape[1]
    operands = (*sources, left, right, coef)
    return pl.pallas_call(
        functools.partial(sent_kernel, first, forward),
        out_shape=(pltpu.VMEM(shape, jnp.bfloat16), pltpu.VMEM(shape, jnp.bfloat16)),
        in_specs=vmem_specs(len(operands)),
        out_specs=tuple(vmem_specs(2)),
        scratch_shapes=scratch(tiles, 4),
        compiler_params=pltpu.CompilerParams(vmem_limit_bytes=GRANT),
        cost_estimate=pl.CostEstimate(flops=1_200_000_000 * tiles, bytes_accessed=4_000_000 * tiles, transcendentals=0),
        name="sent",
    )(*map(in_vmem, operands))


def kept_kernel(*refs):
    sources_a, sources_b, (left, right, coef, own_a, own_b, mixed_a, product_a, mixed_b, product_b) = refs[:3], refs[3:6], refs[6:]
    half = own_a.shape[1]

    def run(first, forward, items, sources, out, mixed, product, t, steps):
        mix(t, forward, steps, (0, 1, 2), items, sources, coef, None, mixed)
        term = multiply(t, first, 2, left, right, mixed, product)
        for i in range(2):
            for part in range(2):
                out[i, t, part] = term[i * 128 : i * 128 + 128, part * 128 : part * 128 + 128]

    both_ways(coef, half, functools.partial(run, 0, True, KEPT_IN, sources_a, own_a, mixed_a, product_a))
    both_ways(coef, own_b.shape[1], functools.partial(run, half, False, KEPT_OUT, sources_b, own_b, mixed_b, product_b))


def kept(sources_a, sources_b, left, right, coef):
    shape_a, shape_b = sources_a[0].shape, sources_b[0].shape
    operands = (*sources_a, *sources_b, left, right, coef)
    return pl.pallas_call(
        kept_kernel,
        out_shape=(pltpu.VMEM(shape_a, jnp.float32), pltpu.VMEM(shape_b, jnp.float32)),
        in_specs=vmem_specs(len(operands)),
        out_specs=tuple(vmem_specs(2)),
        scratch_shapes=scratch(shape_a[1], 2) + scratch(shape_b[1], 2),
        compiler_params=pltpu.CompilerParams(vmem_limit_bytes=GRANT),
        cost_estimate=pl.CostEstimate(flops=2_400_000_000, bytes_accessed=8_000_000, transcendentals=0),
        name="kept",
    )(*map(in_vmem, operands))


def gather_kernel(own, far, coef, out):
    inner = jnp.broadcast_to(coef[INNER][:1] > 0.5, out.shape[-2:])
    for index in itertools.product(*map(range, out.shape[:-2])):
        out[index] = own[index] + jnp.where(inner, far[index].astype(jnp.float32), 0.0)


def gather(own, far, coef):
    return pl.pallas_call(
        gather_kernel,
        out_shape=pltpu.VMEM(own.shape, jnp.float32),
        in_specs=vmem_specs(3),
        out_specs=vmem_specs(1)[0],
        compiler_params=pltpu.CompilerParams(vmem_limit_bytes=GRANT),
        cost_estimate=pl.CostEstimate(flops=1000_000_000, bytes_accessed=1000_000, transcendentals=0),
        name="gather",
    )(in_vmem(own), in_vmem(far), in_vmem(coef))


def finish_kernel(far_a, near_a, near_b, own_a, own_b, out, held, sems):
    tiles_a, tiles_b = own_a.shape[1], own_b.shape[1]
    f32 = jnp.float32
    copies = []
    for t in range(tiles_a + tiles_b):
        if t < tiles_a:
            value = own_a[:, t] + near_a[:, t].astype(f32) + far_a[:, t].astype(f32)
        else:
            value = own_b[:, t - tiles_a] + near_b[:, t - tiles_a].astype(f32)
        held[:, t] = value.astype(held.dtype)
        copies.append(pltpu.make_async_copy(held.at[:, t], out.at[0, :, t], sems.at[t]))
        copies[-1].start()
    for copy in copies:
        copy.wait()


def finish(far_a, near_a, near_b, own_a, own_b):
    e, tiles_a = own_a.shape[:2]
    tiles = tiles_a + own_b.shape[1]
    shape = (e, tiles) + own_a.shape[2:]
    return pl.pallas_call(
        finish_kernel,
        out_shape=jax.ShapeDtypeStruct((1,) + shape, jnp.bfloat16),
        in_specs=vmem_specs(5),
        out_specs=pl.BlockSpec(memory_space=pl.ANY),
        scratch_shapes=[pltpu.VMEM(shape, jnp.bfloat16), pltpu.SemaphoreType.DMA((tiles,))],
        compiler_params=pltpu.CompilerParams(vmem_limit_bytes=GRANT),
        name="finish",
    )(*map(in_vmem, (far_a, near_a, near_b, own_a, own_b)))


def local(green_tiles, dham_blocks, phonon_weight, phonon_modes, tile_pattern):
    n_e, n_k = (lax.axis_size(axis) for axis in AXES)
    route = routes(n_e, n_k)

    def send(block, name):
        return lax.ppermute(block, AXES, route[name])

    tiles = green_tiles[0]
    half = tiles.shape[1] // 2
    in_a, in_b = tiles[:, :half], tiles[:, half:]
    e, k = (lax.axis_index(axis) for axis in AXES)
    inner = (e > 0) & (e < n_e - 1)
    parity = jnp.stack([e % 2, k % 2, inner]).astype(jnp.int32)
    near_a = send(in_a, "pair")
    far_b = send(in_b, "far")
    near_b = send(in_b, "core")
    left, right, coef = prepare(parity, phonon_modes.T, phonon_weight.transpose(1, 2, 0), tile_pattern.T, dham_blocks)
    partial_b = premix(in_b, coef)
    near_a, partial_b = lax.optimization_barrier((near_a, partial_b))
    far_a = send(near_a, "relay")
    far_b, near_a = lax.optimization_barrier((far_b, near_a))
    pair_b, cross_b = sent(half, False, (near_b, far_b, partial_b), left, right, coef)
    cross_b = send(cross_b, "cross")
    core_a, next_a = sent(0, True, (in_a, near_a, far_a), left, right, coef)
    in_b, next_a, pair_b = lax.optimization_barrier((in_b, next_a, pair_b))
    next_a = send(next_a, "far")
    core_a = send(core_a, "core")
    pair_b = send(pair_b, "pair")
    own_a, own_b = kept((in_a, near_a, far_a), (in_b, near_b, far_b), left, right, coef)
    own_b, cross_b = lax.optimization_barrier((own_b, cross_b))
    return finish(next_a, core_a, pair_b, own_a, gather(own_b, cross_b, coef))


def solution(mesh):
    placed = (P("momentum", "energy", None, None, None, None), P(), P(), P(), P())
    return jax.shard_map(
        local,
        mesh=mesh,
        in_specs=placed,
        out_specs=P("momentum", "energy", None, None, None, None),
        check_vma=False,
    )
```

```python
import functools
import itertools
import jax
import jax.numpy as jnp
from jax import lax
from jax.experimental import pallas as pl
from jax.experimental.pallas import tpu as pltpu
from jax.sharding import PartitionSpec as P

AXES = ("energy", "momentum")
DIRS = 3
REACH = 2
EVEN = 3 * DIRS * (2 * REACH + 1)
AT_REST = EVEN + 1
INNER = EVEN + 2
ENTRIES = EVEN + 3
ROWS = 32
GRANT = 16 * 2**20


def in_vmem(array):
    return pltpu.with_memory_space_constraint(array, pltpu.VMEM)


def in_hbm(array):
    return pltpu.with_memory_space_constraint(array, pltpu.HBM)


def vmem_specs(count):
    return [pl.BlockSpec(memory_space=pltpu.VMEM)] * count


def routes(n_e, n_k):
    def pairs(step):
        return [(e * n_k + k, to_e * n_k + to_k % n_k) for e in range(n_e) for k in range(n_k) for to_e, to_k in [step(e, k)]]

    def inside(e, otherwise):
        return e if 0 <= e < n_e else otherwise

    return {
        "pair": pairs(lambda e, k: (e ^ 1, k)),
        "relay": pairs(lambda e, k: (inside(e + 2 - 4 * (e % 2), e ^ 1), k)),
        "cross": pairs(lambda e, k: (inside(e - 1 + 2 * (e % 2), e), k ^ (0 <= e - 1 + 2 * (e % 2) < n_e) ^ 1)),
        "core": pairs(lambda e, k: (e, k ^ 1)),
        "far": pairs(lambda e, k: (e, k - 1 + 2 * (k % 2))),
    }


def prepare_kernel(parity, modes, weight, pattern, dham, left, right, coef, table):
    mode_count = modes.shape[1]
    tile_count = pattern.shape[1]
    for q in range(4):
        for d in range(DIRS):
            for s in range(2 * REACH + 1):
                table[q, d, s] = 0.0
    for m in range(mode_count):
        q = modes[0, m] + 1
        step = modes[1, m]
        for d in range(DIRS):
            table[q, d, REACH - step] = table[q, d, REACH - step] + weight[d, 0, m]
            table[q, d, REACH + step] = table[q, d, REACH + step] + weight[d, 1, m]
    toward = 1 - 2 * parity[1]
    at_rest = 0.0
    for slot, q in enumerate((0, toward, -toward)):
        for d in range(DIRS):
            for s in range(2 * REACH + 1):
                value = table[q + 1, d, s]
                if s == REACH:
                    at_rest = at_rest + jnp.abs(value)
                value = jnp.full((8, 128), value, jnp.float32)
                coef[(slot * DIRS + d) * (2 * REACH + 1) + s] = value.astype(jnp.bfloat16).astype(jnp.float32)
    coef[EVEN] = jnp.full((8, 128), 1 - parity[0], jnp.int32).astype(jnp.float32)
    coef[INNER] = jnp.full((8, 128), parity[2], jnp.int32).astype(jnp.float32)
    coef[AT_REST] = jnp.full((8, 128), at_rest, jnp.float32)
    for t in range(tile_count):
        lo, hi = pattern[0, t], pattern[1, t]
        for d in range(DIRS):
            real, imag = dham[d, lo, 0], dham[d, lo, 1]
            left[t, d, :128, :128] = real
            left[t, d, :128, 128:] = -imag
            left[t, d, 128:, :128] = imag
            left[t, d, 128:, 128:] = real
            real, imag = dham[d, hi, 0].T, dham[d, hi, 1].T
            right[t, d, :128, :128] = real
            right[t, d, :128, 128:] = -imag
            right[t, d, 128:, :128] = imag
            right[t, d, 128:, 128:] = real


def prepare(parity, modes, weight, pattern, dham):
    tile_count = pattern.shape[1]
    big = pltpu.VMEM((tile_count, DIRS, 256, 256), jnp.bfloat16)
    return pl.pallas_call(
        prepare_kernel,
        out_shape=(big, big, pltpu.VMEM((ENTRIES, 8, 128), jnp.float32)),
        in_specs=[pl.BlockSpec(memory_space=pltpu.SMEM)] * 4 + vmem_specs(1),
        out_specs=tuple(vmem_specs(3)),
        scratch_shapes=[pltpu.SMEM((4, DIRS, 2 * REACH + 1), jnp.float32)],
        compiler_params=pltpu.CompilerParams(vmem_limit_bytes=GRANT),
        name="prepare",
    )(parity, in_hbm(modes), in_hbm(weight), in_hbm(pattern), in_hbm(dham))


def mix(t, forward, steps, blocks, items, sources, coef, partial, out):
    even, inner = coef[EVEN] > 0.5, coef[INNER] > 0.5

    def at(slot, d, s):
        return coef[(slot * DIRS + d) * (2 * REACH + 1) + s + REACH]

    for part in range(2):
        for row in range(0, 128, ROWS):

            def load(source, j):
                ref, tile = (source[t], 0) if isinstance(source, list) else (source, t)
                return ref[j, tile, part, pl.ds(row, ROWS), :].astype(jnp.float32).reshape(ROWS // 8, 8, 128)

            taken = {block: [load(sources[block], j) for j in range(2)] for block in blocks}
            if forward:
                taken[2] = [jnp.where(inner, value, 0.0) for value in taken[2]]
                below = [jnp.where(even, b, a) for a, b in zip(taken[1], taken[2])]
                above = [jnp.where(even, a, b) for a, b in zip(taken[1], taken[2])]
                line = below + taken[0] + above
            for d in range(DIRS):
                for at_item, item in enumerate(items):
                    if forward:
                        slot, i = divmod(item, 2)
                        terms = [(line[2 + i + s], at(slot, d, s)) for s in steps]
                    else:
                        place = item - 2
                        terms = [(taken[m][j], at((0, 2, 1)[m], d, j - place)) for m in blocks for j in range(2) if j - place in steps]
                    here = (t, d, pl.ds(part * 128 + row, ROWS), pl.ds(at_item * 128, 128))
                    acc = terms[0][0] * terms[0][1]
                    if partial is not None:
                        acc = acc + partial[here].reshape(ROWS // 8, 8, 128)
                    for value, factor in terms[1:]:
                        acc = acc + value * factor
                    out[here] = acc.reshape(ROWS, 128).astype(out.dtype)


def multiply(t, first, count, left, right, mixed, product):
    for d in range(DIRS):
        got = jnp.dot(left[first + t, d], mixed[t, d], preferred_element_type=jnp.float32).astype(jnp.bfloat16)
        for item in range(count):
            for part in range(2):
                product[t, pl.ds(item * 128, 128), pl.ds(d * 256 + part * 128, 128)] = got[
                    part * 128 : part * 128 + 128, item * 128 : item * 128 + 128
                ]
    return jnp.dot(product[t], right[first + t].reshape(DIRS * 256, 256), preferred_element_type=jnp.float32)


def both_ways(coef, tiles, run):
    at_rest = jnp.max(coef[AT_REST])

    @pl.when(at_rest == 0.0)
    def _():
        for t in range(tiles):
            run(t, (-2, -1, 1, 2))

    @pl.when(at_rest != 0.0)
    def _():
        for t in range(tiles):
            run(t, (-2, -1, 0, 1, 2))


def flat(*sources):
    arrays, places = jax.tree.flatten(sources)
    return arrays, functools.partial(jax.tree.unflatten, places), len(arrays)


def scratch(tiles, count):
    return [
        pltpu.VMEM((tiles, DIRS, 256, count * 128), jnp.bfloat16),
        pltpu.VMEM((tiles, count * 128, DIRS * 256), jnp.bfloat16),
    ]


SENT_IN, SENT_OUT, KEPT_IN, KEPT_OUT = (2, 3, 4, 5), (0, 1, 4, 5), (0, 1), (2, 3)


def premix_kernel(places, count, *refs):
    (own,), (coef, partial) = places(refs[:count]), refs[count:]
    both_ways(coef, partial.shape[0], lambda t, steps: mix(t, False, steps, (0,), SENT_OUT, (own,), coef, None, partial))


def premix(tiles, own, coef):
    arrays, places, count = flat(own)
    return pl.pallas_call(
        functools.partial(premix_kernel, places, count),
        out_shape=pltpu.VMEM((tiles, DIRS, 256, len(SENT_OUT) * 128), jnp.float32),
        in_specs=vmem_specs(count + 1),
        out_specs=vmem_specs(1)[0],
        compiler_params=pltpu.CompilerParams(vmem_limit_bytes=GRANT),
        cost_estimate=pl.CostEstimate(flops=300_000_000 * tiles, bytes_accessed=1_000_000 * tiles, transcendentals=0),
        name="premix",
    )(*map(in_vmem, (*arrays, coef)))


def sent_kernel(first, forward, places, count, *refs):
    sources, (left, right, coef, to_near, to_far, mixed, product) = places(refs[:count]), refs[count:]

    def run(t, steps):
        if forward:
            mix(t, True, steps, (0, 1, 2), SENT_IN, sources, coef, None, mixed)
        else:
            mix(t, False, steps, (1, 2), SENT_OUT, {1: sources[0], 2: sources[1]}, coef, sources[2], mixed)
        term = multiply(t, first, 4, left, right, mixed, product)
        even = jnp.broadcast_to(coef[EVEN][:1] > 0.5, (128, 128))
        for i in range(2):
            for part in range(2):
                one, two = (term[at * 128 : at * 128 + 128, part * 128 : part * 128 + 128] for at in (i, 2 + i))
                if not forward:
                    one, two = jnp.where(even, two, one), jnp.where(even, one, two)
                to_near[i, t, part] = one.astype(to_near.dtype)
                to_far[i, t, part] = two.astype(to_far.dtype)

    both_ways(coef, to_near.shape[1], run)


def sent(first, forward, shape, sources, left, right, coef):
    tiles = shape[1]
    arrays, places, count = flat(*sources)
    return pl.pallas_call(
        functools.partial(sent_kernel, first, forward, places, count),
        out_shape=(pltpu.VMEM(shape, jnp.bfloat16), pltpu.VMEM(shape, jnp.bfloat16)),
        in_specs=vmem_specs(count + 3),
        out_specs=tuple(vmem_specs(2)),
        scratch_shapes=scratch(tiles, 4),
        compiler_params=pltpu.CompilerParams(vmem_limit_bytes=GRANT),
        cost_estimate=pl.CostEstimate(flops=1_200_000_000 * tiles, bytes_accessed=4_000_000 * tiles, transcendentals=0),
        name="sent",
    )(*map(in_vmem, (*arrays, left, right, coef)))


def kept_kernel(places, count, *refs):
    (sources_a, sources_b), rest = places(refs[:count]), refs[count:]
    left, right, coef, own_a, own_b, mixed_a, product_a, mixed_b, product_b = rest
    half = own_a.shape[1]

    def run(first, forward, items, sources, out, mixed, product, t, steps):
        mix(t, forward, steps, (0, 1, 2), items, sources, coef, None, mixed)
        term = multiply(t, first, 2, left, right, mixed, product)
        for i in range(2):
            for part in range(2):
                out[i, t, part] = term[i * 128 : i * 128 + 128, part * 128 : part * 128 + 128]

    both_ways(coef, half, functools.partial(run, 0, True, KEPT_IN, sources_a, own_a, mixed_a, product_a))
    both_ways(coef, own_b.shape[1], functools.partial(run, half, False, KEPT_OUT, sources_b, own_b, mixed_b, product_b))


def kept(shape_a, shape_b, sources_a, sources_b, left, right, coef):
    arrays, places, count = flat(sources_a, sources_b)
    return pl.pallas_call(
        functools.partial(kept_kernel, places, count),
        out_shape=(pltpu.VMEM(shape_a, jnp.float32), pltpu.VMEM(shape_b, jnp.float32)),
        in_specs=vmem_specs(count + 3),
        out_specs=tuple(vmem_specs(2)),
        scratch_shapes=scratch(shape_a[1], 2) + scratch(shape_b[1], 2),
        compiler_params=pltpu.CompilerParams(vmem_limit_bytes=GRANT),
        cost_estimate=pl.CostEstimate(flops=2_400_000_000, bytes_accessed=8_000_000, transcendentals=0),
        name="kept",
    )(*map(in_vmem, (*arrays, left, right, coef)))


def gather_kernel(far, near, coef, out):
    inner = jnp.broadcast_to(coef[INNER][:1] > 0.5, out.shape[-2:])
    for index in itertools.product(*map(range, out.shape[:-2])):
        out[index] = near[index].astype(jnp.float32) + jnp.where(inner, far[index].astype(jnp.float32), 0.0)


def gather(near, far, coef):
    return pl.pallas_call(
        gather_kernel,
        out_shape=pltpu.VMEM(near.shape, jnp.float32),
        in_specs=vmem_specs(3),
        out_specs=vmem_specs(1)[0],
        compiler_params=pltpu.CompilerParams(vmem_limit_bytes=GRANT),
        cost_estimate=pl.CostEstimate(flops=1000_000_000, bytes_accessed=1000_000, transcendentals=0),
        name="gather",
    )(in_vmem(far), in_vmem(near), in_vmem(coef))


def finish_kernel(own_a, near_a, far_a, own_b, from_b, out, held, sems):
    tiles_a, tiles_b = own_a.shape[1], own_b.shape[1]
    f32 = jnp.float32
    copies = []
    for t in range(tiles_a + tiles_b):
        if t < tiles_a:
            value = own_a[:, t] + near_a[:, t].astype(f32) + far_a[:, t].astype(f32)
        else:
            value = own_b[:, t - tiles_a] + from_b[:, t - tiles_a]
        held[:, t] = value.astype(held.dtype)
        copies.append(pltpu.make_async_copy(held.at[:, t], out.at[0, :, t], sems.at[t]))
        copies[-1].start()
    for copy in copies:
        copy.wait()


def finish(own_a, near_a, far_a, own_b, from_b):
    e, tiles_a = own_a.shape[:2]
    tiles = tiles_a + own_b.shape[1]
    shape = (e, tiles) + own_a.shape[2:]
    return pl.pallas_call(
        finish_kernel,
        out_shape=jax.ShapeDtypeStruct((1,) + shape, jnp.bfloat16),
        in_specs=vmem_specs(5),
        out_specs=pl.BlockSpec(memory_space=pl.ANY),
        scratch_shapes=[pltpu.VMEM(shape, jnp.bfloat16), pltpu.SemaphoreType.DMA((tiles,))],
        compiler_params=pltpu.CompilerParams(vmem_limit_bytes=GRANT),
        name="finish",
    )(*map(in_vmem, (own_a, near_a, far_a, own_b, from_b)))


def split_kernel(source, *refs):
    outs, sems = refs[:-1], refs[-1]
    copies, tile = [], 0
    for at, out in enumerate(outs):
        copies.append(pltpu.make_async_copy(source.at[0, :, pl.ds(tile, out.shape[1])], out, sems.at[at]))
        copies[-1].start()
        tile += out.shape[1]
    for copy in copies:
        copy.wait()


def split(tiles, counts):
    _, e, _, *rest = tiles.shape
    return pl.pallas_call(
        split_kernel,
        out_shape=tuple(pltpu.VMEM((e, count, *rest), tiles.dtype) for count in counts),
        in_specs=[pl.BlockSpec(memory_space=pltpu.HBM)],
        out_specs=tuple(vmem_specs(len(counts))),
        scratch_shapes=[pltpu.SemaphoreType.DMA((len(counts),))],
        compiler_params=pltpu.CompilerParams(vmem_limit_bytes=GRANT),
        name="split",
    )(in_hbm(tiles))


def local(green_tiles, dham_blocks, phonon_weight, phonon_modes, tile_pattern):
    n_e, n_k = (lax.axis_size(axis) for axis in AXES)
    route = routes(n_e, n_k)

    def send(block, name):
        return lax.ppermute(block, AXES, route[name])

    tiles = green_tiles[0]
    half = tiles.shape[1] // 2
    e_count, tile_count, *rest = tiles.shape
    shape_a, shape_b = (e_count, half, *rest), (e_count, tile_count - half, *rest)
    *in_a, in_b = split(green_tiles, [1] * half + [tile_count - half])
    e, k = (lax.axis_index(axis) for axis in AXES)
    inner = (e > 0) & (e < n_e - 1)
    parity = jnp.stack([e % 2, k % 2, inner]).astype(jnp.int32)
    near_a = [send(block, "pair") for block in in_a]
    far_b = send(in_b, "far")
    near_b = send(in_b, "core")
    left, right, coef = prepare(parity, phonon_modes.T, phonon_weight.transpose(1, 2, 0), tile_pattern.T, dham_blocks)
    partial_b = premix(shape_b[1], in_b, coef)
    near_a[0], partial_b = lax.optimization_barrier((near_a[0], partial_b))
    far_a = [send(block, "relay") for block in near_a]
    far_b, near_a = lax.optimization_barrier((far_b, near_a))
    pair_b, cross_b = sent(half, False, shape_b, (near_b, far_b, partial_b), left, right, coef)
    cross_b = send(cross_b, "cross")
    pair_b = send(pair_b, "pair")
    core_a, next_a = sent(0, True, shape_a, (in_a, near_a, far_a), left, right, coef)
    in_b, next_a = lax.optimization_barrier((in_b, next_a))
    core_a = send(core_a, "core")
    next_a = send(next_a, "far")
    own_a, own_b = kept(shape_a, shape_b, (in_a, near_a, far_a), (in_b, near_b, far_b), left, right, coef)
    own_b, pair_b = lax.optimization_barrier((own_b, pair_b))
    return finish(own_a, core_a, next_a, own_b, gather(pair_b, cross_b, coef))


def solution(mesh):
    placed = (P("momentum", "energy", None, None, None, None), P(), P(), P(), P())
    return jax.shard_map(
        local,
        mesh=mesh,
        in_specs=placed,
        out_specs=P("momentum", "energy", None, None, None, None),
        check_vma=False,
    )
```

```python
import functools
import itertools
import jax
import jax.numpy as jnp
from jax import lax
from jax.experimental import pallas as pl
from jax.experimental.pallas import tpu as pltpu
from jax.sharding import PartitionSpec as P

AXES = ("energy", "momentum")
DIRS = 3
REACH = 2
EVEN = 3 * DIRS * (2 * REACH + 1)
AT_REST = EVEN + 1
INNER = EVEN + 2
OWN_ON = EVEN + 3
ENTRIES = EVEN + 4
ROWS = 32
GRANT = 16 * 2**20


def in_vmem(array):
    return pltpu.with_memory_space_constraint(array, pltpu.VMEM)


def in_hbm(array):
    return pltpu.with_memory_space_constraint(array, pltpu.HBM)


def vmem_specs(count):
    return [pl.BlockSpec(memory_space=pltpu.VMEM)] * count


def routes(n_e, n_k):
    def pairs(step):
        return [(e * n_k + k, to_e * n_k + to_k % n_k) for e in range(n_e) for k in range(n_k) for to_e, to_k in [step(e, k)]]

    def relay(e, k):
        if e in (0, n_e - 1):
            return e, k ^ 1
        if e in (1, n_e - 2):
            return (2 if e == 1 else n_e - 3), k
        return e + 2 - 4 * (e % 2), k

    def ring(e, k):
        to_e = e + 2 - 4 * (e % 2)
        return (to_e if 0 <= to_e < n_e else e ^ 1), k

    def cross(e, k):
        to_e = e - 1 + 2 * (e % 2)
        return (to_e, k) if 0 <= to_e < n_e else (e, k ^ 1)

    return {
        "pair": pairs(lambda e, k: (e ^ 1, k)),
        "relay": pairs(relay),
        "ring": pairs(ring),
        "cross": pairs(cross),
        "core": pairs(lambda e, k: (e, k ^ 1)),
        "far": pairs(lambda e, k: (e, k - 1 + 2 * (k % 2))),
    }


def prepare_kernel(parity, modes, weight, pattern, dham, left, right, coef, table):
    mode_count = modes.shape[1]
    tile_count = pattern.shape[1]
    for q in range(4):
        for d in range(DIRS):
            for s in range(2 * REACH + 1):
                table[q, d, s] = 0.0
    for m in range(mode_count):
        q = modes[0, m] + 1
        step = modes[1, m]
        for d in range(DIRS):
            table[q, d, REACH - step] = table[q, d, REACH - step] + weight[d, 0, m]
            table[q, d, REACH + step] = table[q, d, REACH + step] + weight[d, 1, m]
    toward = 1 - 2 * parity[1]
    at_rest = 0.0
    for slot, q in enumerate((0, toward, -toward)):
        for d in range(DIRS):
            for s in range(2 * REACH + 1):
                value = table[q + 1, d, s]
                if s == REACH:
                    at_rest = at_rest + jnp.abs(value)
                value = jnp.full((8, 128), value, jnp.float32)
                coef[(slot * DIRS + d) * (2 * REACH + 1) + s] = value.astype(jnp.bfloat16).astype(jnp.float32)
    coef[EVEN] = jnp.full((8, 128), 1 - parity[0], jnp.int32).astype(jnp.float32)
    coef[INNER] = jnp.full((8, 128), parity[2], jnp.int32).astype(jnp.float32)
    coef[OWN_ON] = jnp.full((8, 128), parity[3], jnp.int32).astype(jnp.float32)
    coef[AT_REST] = jnp.full((8, 128), at_rest, jnp.float32)
    for t in range(tile_count):
        lo, hi = pattern[0, t], pattern[1, t]
        for d in range(DIRS):
            real, imag = dham[d, lo, 0], dham[d, lo, 1]
            left[t, d, :128, :128] = real
            left[t, d, :128, 128:] = -imag
            left[t, d, 128:, :128] = imag
            left[t, d, 128:, 128:] = real
            real, imag = dham[d, hi, 0].T, dham[d, hi, 1].T
            right[t, d, :128, :128] = real
            right[t, d, :128, 128:] = -imag
            right[t, d, 128:, :128] = imag
            right[t, d, 128:, 128:] = real


def prepare(parity, modes, weight, pattern, dham):
    tile_count = pattern.shape[1]
    big = pltpu.VMEM((tile_count, DIRS, 256, 256), jnp.bfloat16)
    return pl.pallas_call(
        prepare_kernel,
        out_shape=(big, big, pltpu.VMEM((ENTRIES, 8, 128), jnp.float32)),
        in_specs=[pl.BlockSpec(memory_space=pltpu.SMEM)] * 4 + vmem_specs(1),
        out_specs=tuple(vmem_specs(3)),
        scratch_shapes=[pltpu.SMEM((4, DIRS, 2 * REACH + 1), jnp.float32)],
        compiler_params=pltpu.CompilerParams(vmem_limit_bytes=GRANT),
        name="prepare",
    )(parity, in_hbm(modes), in_hbm(weight), in_hbm(pattern), in_hbm(dham))


def mix(t, forward, steps, blocks, items, sources, coef, partial, out):
    even, inner = coef[EVEN] > 0.5, coef[INNER] > 0.5

    def at(slot, d, s):
        return coef[(slot * DIRS + d) * (2 * REACH + 1) + s + REACH]

    for part in range(2):
        for row in range(0, 128, ROWS):

            def load(source, j):
                ref, tile = (source[t], 0) if isinstance(source, list) else (source, t)
                return ref[j, tile, part, pl.ds(row, ROWS), :].astype(jnp.float32).reshape(ROWS // 8, 8, 128)

            taken = {block: [load(sources[block], j) for j in range(2)] for block in blocks}
            if forward:
                taken[2] = [jnp.where(inner, value, 0.0) for value in taken[2]]
                below = [jnp.where(even, b, a) for a, b in zip(taken[1], taken[2])]
                above = [jnp.where(even, a, b) for a, b in zip(taken[1], taken[2])]
                line = below + taken[0] + above
            for d in range(DIRS):
                for at_item, item in enumerate(items):
                    if forward:
                        slot, i = divmod(item, 2)
                        terms = [(line[2 + i + s], at(slot, d, s)) for s in steps]
                    else:
                        place = item - 2
                        terms = [(taken[m][j], at((0, 2, 1)[m], d, j - place)) for m in blocks for j in range(2) if j - place in steps]
                    here = (t, d, pl.ds(part * 128 + row, ROWS), pl.ds(at_item * 128, 128))
                    acc = terms[0][0] * terms[0][1]
                    if partial is not None:
                        acc = acc + partial[here].reshape(ROWS // 8, 8, 128)
                    for value, factor in terms[1:]:
                        acc = acc + value * factor
                    out[here] = acc.reshape(ROWS, 128).astype(out.dtype)


def multiply(t, first, count, left, right, mixed, product):
    for d in range(DIRS):
        got = jnp.dot(left[first + t, d], mixed[t, d], preferred_element_type=jnp.float32).astype(jnp.bfloat16)
        for item in range(count):
            for part in range(2):
                product[t, pl.ds(item * 128, 128), pl.ds(d * 256 + part * 128, 128)] = got[
                    part * 128 : part * 128 + 128, item * 128 : item * 128 + 128
                ]
    return jnp.dot(product[t], right[first + t].reshape(DIRS * 256, 256), preferred_element_type=jnp.float32)


def both_ways(coef, tiles, run):
    at_rest = jnp.max(coef[AT_REST])

    @pl.when(at_rest == 0.0)
    def _():
        for t in range(tiles):
            run(t, (-2, -1, 1, 2))

    @pl.when(at_rest != 0.0)
    def _():
        for t in range(tiles):
            run(t, (-2, -1, 0, 1, 2))


def flat(*sources):
    arrays, places = jax.tree.flatten(sources)
    return arrays, functools.partial(jax.tree.unflatten, places), len(arrays)


def scratch(tiles, count):
    return [
        pltpu.VMEM((tiles, DIRS, 256, count * 128), jnp.bfloat16),
        pltpu.VMEM((tiles, count * 128, DIRS * 256), jnp.bfloat16),
    ]


SENT_IN, SENT_OUT, KEPT_IN, KEPT_OUT = (2, 3, 4, 5), (0, 1, 4, 5), (0, 1), (2, 3)


def premix_kernel(places, count, *refs):
    (own,), (coef, partial) = places(refs[:count]), refs[count:]
    both_ways(coef, partial.shape[0], lambda t, steps: mix(t, False, steps, (0,), SENT_OUT, (own,), coef, None, partial))


def premix(tiles, own, coef):
    arrays, places, count = flat(own)
    return pl.pallas_call(
        functools.partial(premix_kernel, places, count),
        out_shape=pltpu.VMEM((tiles, DIRS, 256, len(SENT_OUT) * 128), jnp.float32),
        in_specs=vmem_specs(count + 1),
        out_specs=vmem_specs(1)[0],
        compiler_params=pltpu.CompilerParams(vmem_limit_bytes=GRANT),
        cost_estimate=pl.CostEstimate(flops=300_000_000 * tiles, bytes_accessed=1_000_000 * tiles, transcendentals=0),
        name="premix",
    )(*map(in_vmem, (*arrays, coef)))


def sent_kernel(first, forward, places, count, *refs):
    sources, (left, right, coef, to_near, to_far, mixed, product) = places(refs[:count]), refs[count:]

    def run(t, steps):
        if forward:
            mix(t, True, steps, (0, 1, 2), SENT_IN, sources, coef, None, mixed)
        else:
            mix(t, False, steps, (1, 2), SENT_OUT, {1: sources[0], 2: sources[1]}, coef, sources[2], mixed)
        term = multiply(t, first, 4, left, right, mixed, product)
        even = jnp.broadcast_to(coef[EVEN][:1] > 0.5, (128, 128))
        for i in range(2):
            for part in range(2):
                one, two = (term[at * 128 : at * 128 + 128, part * 128 : part * 128 + 128] for at in (i, 2 + i))
                if not forward:
                    one, two = jnp.where(even, two, one), jnp.where(even, one, two)
                to_near[i, t, part] = one.astype(to_near.dtype)
                to_far[i, t, part] = two.astype(to_far.dtype)

    both_ways(coef, to_near.shape[1], run)


def sent(first, forward, shape, sources, left, right, coef):
    tiles = shape[1]
    arrays, places, count = flat(*sources)
    return pl.pallas_call(
        functools.partial(sent_kernel, first, forward, places, count),
        out_shape=(pltpu.VMEM(shape, jnp.bfloat16), pltpu.VMEM(shape, jnp.bfloat16)),
        in_specs=vmem_specs(count + 3),
        out_specs=tuple(vmem_specs(2)),
        scratch_shapes=scratch(tiles, 4),
        compiler_params=pltpu.CompilerParams(vmem_limit_bytes=GRANT),
        cost_estimate=pl.CostEstimate(flops=1_200_000_000 * tiles, bytes_accessed=4_000_000 * tiles, transcendentals=0),
        name="sent",
    )(*map(in_vmem, (*arrays, left, right, coef)))


def kept_kernel(places, count, *refs):
    (sources_a, sources_b), rest = places(refs[:count]), refs[count:]
    left, right, coef, own_a, own_b, mixed_a, product_a, mixed_b, product_b = rest
    half = own_a.shape[1]

    def run(first, forward, items, sources, out, mixed, product, t, steps):
        mix(t, forward, steps, (0, 1, 2), items, sources, coef, None, mixed)
        term = multiply(t, first, 2, left, right, mixed, product)
        for i in range(2):
            for part in range(2):
                out[i, t, part] = term[i * 128 : i * 128 + 128, part * 128 : part * 128 + 128]

    both_ways(coef, half, functools.partial(run, 0, True, KEPT_IN, sources_a, own_a, mixed_a, product_a))
    both_ways(coef, own_b.shape[1], functools.partial(run, half, False, KEPT_OUT, sources_b, own_b, mixed_b, product_b))


def kept(shape_a, shape_b, sources_a, sources_b, left, right, coef):
    arrays, places, count = flat(sources_a, sources_b)
    return pl.pallas_call(
        functools.partial(kept_kernel, places, count),
        out_shape=(pltpu.VMEM(shape_a, jnp.float32), pltpu.VMEM(shape_b, jnp.float32)),
        in_specs=vmem_specs(count + 3),
        out_specs=tuple(vmem_specs(2)),
        scratch_shapes=scratch(shape_a[1], 2) + scratch(shape_b[1], 2),
        compiler_params=pltpu.CompilerParams(vmem_limit_bytes=GRANT),
        cost_estimate=pl.CostEstimate(flops=2_400_000_000, bytes_accessed=8_000_000, transcendentals=0),
        name="kept",
    )(*map(in_vmem, (*arrays, left, right, coef)))


def gather_kernel(far, near, coef, out):
    inner = jnp.broadcast_to(coef[INNER][:1] > 0.5, out.shape[-2:])
    for index in itertools.product(*map(range, out.shape[:-2])):
        out[index] = near[index].astype(jnp.float32) + jnp.where(inner, far[index].astype(jnp.float32), 0.0)


def gather(near, far, coef):
    return pl.pallas_call(
        gather_kernel,
        out_shape=pltpu.VMEM(near.shape, jnp.float32),
        in_specs=vmem_specs(3),
        out_specs=vmem_specs(1)[0],
        compiler_params=pltpu.CompilerParams(vmem_limit_bytes=GRANT),
        cost_estimate=pl.CostEstimate(flops=1000_000_000, bytes_accessed=1000_000, transcendentals=0),
        name="gather",
    )(in_vmem(far), in_vmem(near), in_vmem(coef))


def finish_kernel(own_a, near_a, far_a, own_b, from_b, out, held, sems):
    tiles_a, tiles_b = own_a.shape[1], own_b.shape[1]
    f32 = jnp.float32
    copies = []
    for t in range(tiles_a + tiles_b):
        if t < tiles_a:
            value = own_a[:, t] + near_a[:, t].astype(f32) + far_a[:, t].astype(f32)
        else:
            value = own_b[:, t - tiles_a] + from_b[:, t - tiles_a]
        held[:, t] = value.astype(held.dtype)
        copies.append(pltpu.make_async_copy(held.at[:, t], out.at[0, :, t], sems.at[t]))
        copies[-1].start()
    for copy in copies:
        copy.wait()


def finish(own_a, near_a, far_a, own_b, from_b):
    e, tiles_a = own_a.shape[:2]
    tiles = tiles_a + own_b.shape[1]
    shape = (e, tiles) + own_a.shape[2:]
    return pl.pallas_call(
        finish_kernel,
        out_shape=jax.ShapeDtypeStruct((1,) + shape, jnp.bfloat16),
        in_specs=vmem_specs(5),
        out_specs=pl.BlockSpec(memory_space=pl.ANY),
        scratch_shapes=[pltpu.VMEM(shape, jnp.bfloat16), pltpu.SemaphoreType.DMA((tiles,))],
        compiler_params=pltpu.CompilerParams(vmem_limit_bytes=GRANT),
        name="finish",
    )(*map(in_vmem, (own_a, near_a, far_a, own_b, from_b)))


def choose_kernel(own, near, coef, out):
    first = jnp.broadcast_to(coef[OWN_ON][:1] > 0.5, out.shape[-2:])
    for index in itertools.product(*map(range, out.shape[:-2])):
        mine, other = own[index].astype(jnp.float32), near[index].astype(jnp.float32)
        out[index] = jnp.where(first, mine, other).astype(out.dtype)


def choose(own, near, coef):
    return pl.pallas_call(
        choose_kernel,
        out_shape=pltpu.VMEM(own.shape, own.dtype),
        in_specs=vmem_specs(3),
        out_specs=vmem_specs(1)[0],
        compiler_params=pltpu.CompilerParams(vmem_limit_bytes=GRANT),
        name="choose",
    )(in_vmem(own), in_vmem(near), in_vmem(coef))


def split_kernel(source, *refs):
    outs, sems = refs[:-1], refs[-1]
    copies, tile = [], 0
    for at, out in enumerate(outs):
        copies.append(pltpu.make_async_copy(source.at[0, :, pl.ds(tile, out.shape[1])], out, sems.at[at]))
        copies[-1].start()
        tile += out.shape[1]
    for copy in copies:
        copy.wait()


def split(tiles, counts):
    _, e, _, *rest = tiles.shape
    return pl.pallas_call(
        split_kernel,
        out_shape=tuple(pltpu.VMEM((e, count, *rest), tiles.dtype) for count in counts),
        in_specs=[pl.BlockSpec(memory_space=pltpu.HBM)],
        out_specs=tuple(vmem_specs(len(counts))),
        scratch_shapes=[pltpu.SemaphoreType.DMA((len(counts),))],
        compiler_params=pltpu.CompilerParams(vmem_limit_bytes=GRANT),
        name="split",
    )(in_hbm(tiles))


def local(green_tiles, dham_blocks, phonon_weight, phonon_modes, tile_pattern):
    n_e, n_k = (lax.axis_size(axis) for axis in AXES)
    route = routes(n_e, n_k)

    def send(block, name):
        return lax.ppermute(block, AXES, route[name])

    tiles = green_tiles[0]
    half = tiles.shape[1] // 2
    e_count, tile_count, *rest = tiles.shape
    shape_a, shape_b = (e_count, half, *rest), (e_count, tile_count - half, *rest)
    *in_a, in_b = split(green_tiles, [1] * half + [tile_count - half])
    e, k = (lax.axis_index(axis) for axis in AXES)
    inner = (e > 0) & (e < n_e - 1)
    parity = jnp.stack([e % 2, k % 2, inner, (e == 1) | (e == n_e - 2)]).astype(jnp.int32)
    near_a = [send(block, "pair") for block in in_a]
    far_b = send(in_b, "far")
    near_b = send(in_b, "core")
    left, right, coef = prepare(parity, phonon_modes.T, phonon_weight.transpose(1, 2, 0), tile_pattern.T, dham_blocks)
    partial_b = premix(shape_b[1], in_b, coef)
    near_a[0], partial_b = lax.optimization_barrier((near_a[0], partial_b))
    cut = half // 2
    far_a = [send(choose(own, near, coef), "relay") for own, near in zip(in_a[:cut], near_a[:cut])]
    far_a += [send(near, "ring") for near in near_a[cut:]]
    far_b, near_a = lax.optimization_barrier((far_b, near_a))
    pair_b, cross_b = sent(half, False, shape_b, (near_b, far_b, partial_b), left, right, coef)
    cross_b = send(cross_b, "cross")
    pair_b = send(pair_b, "pair")
    core_a, next_a = sent(0, True, shape_a, (in_a, near_a, far_a), left, right, coef)
    in_b, next_a = lax.optimization_barrier((in_b, next_a))
    core_a = send(core_a, "core")
    next_a = send(next_a, "far")
    own_a, own_b = kept(shape_a, shape_b, (in_a, near_a, far_a), (in_b, near_b, far_b), left, right, coef)
    own_b, pair_b = lax.optimization_barrier((own_b, pair_b))
    return finish(own_a, core_a, next_a, own_b, gather(pair_b, cross_b, coef))


def solution(mesh):
    placed = (P("momentum", "energy", None, None, None, None), P(), P(), P(), P())
    return jax.shard_map(
        local,
        mesh=mesh,
        in_specs=placed,
        out_specs=P("momentum", "energy", None, None, None, None),
        check_vma=False,
    )
```

```python
import functools
import itertools
import jax
import jax.numpy as jnp
from jax import lax
from jax.experimental import pallas as pl
from jax.experimental.pallas import tpu as pltpu
from jax.sharding import PartitionSpec as P

AXES = ("energy", "momentum")
DIRS = 3
REACH = 2
EVEN = 3 * DIRS * (2 * REACH + 1)
AT_REST = EVEN + 1
INNER = EVEN + 2
OWN_ON = EVEN + 3
ENTRIES = EVEN + 4
ROWS = 32
GRANT = 16 * 2**20


def in_vmem(array):
    return pltpu.with_memory_space_constraint(array, pltpu.VMEM)


def in_hbm(array):
    return pltpu.with_memory_space_constraint(array, pltpu.HBM)


def vmem_specs(count):
    return [pl.BlockSpec(memory_space=pltpu.VMEM)] * count


def routes(n_e, n_k):
    def pairs(step):
        return [(e * n_k + k, to_e * n_k + to_k % n_k) for e in range(n_e) for k in range(n_k) for to_e, to_k in [step(e, k)]]

    def relay(e, k):
        if e in (0, n_e - 1):
            return e, k ^ 1
        if e in (1, n_e - 2):
            return (2 if e == 1 else n_e - 3), k
        return e + 2 - 4 * (e % 2), k

    def ring(e, k):
        to_e = e + 2 - 4 * (e % 2)
        return (to_e if 0 <= to_e < n_e else e ^ 1), k

    def cross(e, k):
        to_e = e - 1 + 2 * (e % 2)
        return (to_e, k) if 0 <= to_e < n_e else (e, k ^ 1)

    return {
        "pair": pairs(lambda e, k: (e ^ 1, k)),
        "relay": pairs(relay),
        "ring": pairs(ring),
        "cross": pairs(cross),
        "core": pairs(lambda e, k: (e, k ^ 1)),
        "far": pairs(lambda e, k: (e, k - 1 + 2 * (k % 2))),
    }


def prepare_kernel(parity, modes, weight, pattern, dham, left, right, coef, wide, table):
    mode_count = modes.shape[1]
    tile_count = pattern.shape[1]
    for q in range(4):
        for d in range(DIRS):
            for s in range(2 * REACH + 1):
                table[q, d, s] = 0.0
    for m in range(mode_count):
        q = modes[0, m] + 1
        step = modes[1, m]
        for d in range(DIRS):
            table[q, d, REACH - step] = table[q, d, REACH - step] + weight[d, 0, m]
            table[q, d, REACH + step] = table[q, d, REACH + step] + weight[d, 1, m]
    toward = 1 - 2 * parity[1]
    at_rest = 0.0
    for slot, q in enumerate((0, toward, -toward)):
        for d in range(DIRS):
            for s in range(2 * REACH + 1):
                value = table[q + 1, d, s]
                if s == REACH:
                    at_rest = at_rest + jnp.abs(value)
                value = jnp.full((8, 128), value, jnp.float32)
                coef[(slot * DIRS + d) * (2 * REACH + 1) + s] = value.astype(jnp.bfloat16).astype(jnp.float32)
    for slot, q in enumerate((0, toward, -toward)):
        for d in range(DIRS):
            for at in range(2 * REACH + 1):
                value = jnp.full((8, 256), table[q + 1, d, at], jnp.float32)
                wide[(slot * DIRS + d) * (2 * REACH + 1) + at] = value.astype(jnp.bfloat16)
    wide[EVEN] = jnp.full((8, 256), 1 - parity[0], jnp.int32).astype(jnp.float32).astype(jnp.bfloat16)
    wide[INNER] = jnp.full((8, 256), parity[2], jnp.int32).astype(jnp.float32).astype(jnp.bfloat16)
    coef[EVEN] = jnp.full((8, 128), 1 - parity[0], jnp.int32).astype(jnp.float32)
    coef[INNER] = jnp.full((8, 128), parity[2], jnp.int32).astype(jnp.float32)
    coef[OWN_ON] = jnp.full((8, 128), parity[3], jnp.int32).astype(jnp.float32)
    coef[AT_REST] = jnp.full((8, 128), at_rest, jnp.float32)
    for t in range(tile_count):
        lo, hi = pattern[0, t], pattern[1, t]
        for d in range(DIRS):
            real, imag = dham[d, lo, 0], dham[d, lo, 1]
            left[t, d, :128, :128] = real
            left[t, d, :128, 128:] = -imag
            left[t, d, 128:, :128] = imag
            left[t, d, 128:, 128:] = real
            real, imag = dham[d, hi, 0].T, dham[d, hi, 1].T
            right[t, d, :128, :128] = real
            right[t, d, :128, 128:] = -imag
            right[t, d, 128:, :128] = imag
            right[t, d, 128:, 128:] = real


def prepare(parity, modes, weight, pattern, dham):
    tile_count = pattern.shape[1]
    big = pltpu.VMEM((tile_count, DIRS, 256, 256), jnp.bfloat16)
    return pl.pallas_call(
        prepare_kernel,
        out_shape=(big, big, pltpu.VMEM((ENTRIES, 8, 128), jnp.float32), pltpu.VMEM((ENTRIES, 8, 256), jnp.bfloat16)),
        in_specs=[pl.BlockSpec(memory_space=pltpu.SMEM)] * 4 + vmem_specs(1),
        out_specs=tuple(vmem_specs(4)),
        scratch_shapes=[pltpu.SMEM((4, DIRS, 2 * REACH + 1), jnp.float32)],
        compiler_params=pltpu.CompilerParams(vmem_limit_bytes=GRANT),
        name="prepare",
    )(parity, in_hbm(modes), in_hbm(weight), in_hbm(pattern), in_hbm(dham))


def mix(t, forward, steps, blocks, items, sources, coef, partial, out):
    even, inner = coef[EVEN] > 0.5, coef[INNER] > 0.5

    def at(slot, d, s):
        return coef[(slot * DIRS + d) * (2 * REACH + 1) + s + REACH]

    for part in range(2):
        for row in range(0, 128, ROWS):

            def load(source, j):
                ref, tile = (source[t], 0) if isinstance(source, list) else (source, t)
                return ref[j, tile, part, pl.ds(row, ROWS), :].astype(jnp.float32).reshape(ROWS // 8, 8, 128)

            taken = {block: [load(sources[block], j) for j in range(2)] for block in blocks}
            if forward:
                taken[2] = [jnp.where(inner, value, 0.0) for value in taken[2]]
                below = [jnp.where(even, b, a) for a, b in zip(taken[1], taken[2])]
                above = [jnp.where(even, a, b) for a, b in zip(taken[1], taken[2])]
                line = below + taken[0] + above
            for d in range(DIRS):
                for at_item, item in enumerate(items):
                    if forward:
                        slot, i = divmod(item, 2)
                        terms = [(line[2 + i + s], at(slot, d, s)) for s in steps]
                    else:
                        place = item - 2
                        terms = [(taken[m][j], at((0, 2, 1)[m], d, j - place)) for m in blocks for j in range(2) if j - place in steps]
                    here = (t, d, pl.ds(part * 128 + row, ROWS), pl.ds(at_item * 128, 128))
                    acc = terms[0][0] * terms[0][1]
                    if partial is not None:
                        acc = acc + partial[here].reshape(ROWS // 8, 8, 128)
                    for value, factor in terms[1:]:
                        acc = acc + value * factor
                    out[here] = acc.reshape(ROWS, 128).astype(out.dtype)


def mix_wide(t, steps, sources, wide, mixed):
    even, inner = wide[EVEN] > 0.5, wide[INNER] > 0.5
    for part in range(2):
        for row in range(0, 128, ROWS):
            own, near, far = (
                jnp.concatenate([source[t][j, 0, part, pl.ds(row, ROWS), :] for j in range(2)], axis=1).reshape(ROWS // 8, 8, 256)
                for source in sources
            )
            far = jnp.where(inner, far, jnp.zeros_like(far))
            below, above = jnp.where(even, far, near), jnp.where(even, near, far)
            beside = {
                -2: below,
                -1: jnp.concatenate([below[..., 128:], own[..., :128]], axis=2),
                0: own,
                1: jnp.concatenate([own[..., 128:], above[..., :128]], axis=2),
                2: above,
            }
            for d in range(DIRS):
                for slot in (1, 2):
                    terms = [beside[s] * wide[(slot * DIRS + d) * (2 * REACH + 1) + s + REACH] for s in steps]
                    while len(terms) > 1:
                        terms = [a + b for a, b in zip(terms[::2], terms[1::2])] + terms[len(terms) - len(terms) % 2 :]
                    mixed[t, d, pl.ds(part * 128 + row, ROWS), pl.ds(slot * 256 - 256, 256)] = terms[0].reshape(ROWS, 256)


def multiply(t, first, count, left, right, mixed, product):
    for d in range(DIRS):
        got = jnp.dot(left[first + t, d], mixed[t, d], preferred_element_type=jnp.float32).astype(jnp.bfloat16)
        for item in range(count):
            for part in range(2):
                product[t, pl.ds(item * 128, 128), pl.ds(d * 256 + part * 128, 128)] = got[
                    part * 128 : part * 128 + 128, item * 128 : item * 128 + 128
                ]
    return jnp.dot(product[t], right[first + t].reshape(DIRS * 256, 256), preferred_element_type=jnp.float32)


def both_ways(coef, tiles, run):
    at_rest = jnp.max(coef[AT_REST])

    @pl.when(at_rest == 0.0)
    def _():
        for t in range(tiles):
            run(t, (-2, -1, 1, 2))

    @pl.when(at_rest != 0.0)
    def _():
        for t in range(tiles):
            run(t, (-2, -1, 0, 1, 2))


def flat(*sources):
    arrays, places = jax.tree.flatten(sources)
    return arrays, functools.partial(jax.tree.unflatten, places), len(arrays)


def scratch(tiles, count):
    return [
        pltpu.VMEM((tiles, DIRS, 256, count * 128), jnp.bfloat16),
        pltpu.VMEM((tiles, count * 128, DIRS * 256), jnp.bfloat16),
    ]


SENT_IN, SENT_OUT, KEPT_IN, KEPT_OUT = (2, 3, 4, 5), (0, 1, 4, 5), (0, 1), (2, 3)


def premix_kernel(places, count, *refs):
    (own,), (coef, partial) = places(refs[:count]), refs[count:]
    both_ways(coef, partial.shape[0], lambda t, steps: mix(t, False, steps, (0,), SENT_OUT, (own,), coef, None, partial))


def premix(tiles, own, coef):
    arrays, places, count = flat(own)
    return pl.pallas_call(
        functools.partial(premix_kernel, places, count),
        out_shape=pltpu.VMEM((tiles, DIRS, 256, len(SENT_OUT) * 128), jnp.float32),
        in_specs=vmem_specs(count + 1),
        out_specs=vmem_specs(1)[0],
        compiler_params=pltpu.CompilerParams(vmem_limit_bytes=GRANT),
        cost_estimate=pl.CostEstimate(flops=300_000_000 * tiles, bytes_accessed=1_000_000 * tiles, transcendentals=0),
        name="premix",
    )(*map(in_vmem, (*arrays, coef)))


def sent_kernel(first, forward, places, count, *refs):
    sources, (left, right, coef, to_near, to_far, mixed, product) = places(refs[:count]), refs[count:]

    def run(t, steps):
        if forward:
            mix_wide(t, steps, sources[:3], sources[3], mixed)
        else:
            mix(t, False, steps, (1, 2), SENT_OUT, {1: sources[0], 2: sources[1]}, coef, sources[2], mixed)
        term = multiply(t, first, 4, left, right, mixed, product)
        even = jnp.broadcast_to(coef[EVEN][:1] > 0.5, (128, 128))
        for i in range(2):
            for part in range(2):
                one, two = (term[at * 128 : at * 128 + 128, part * 128 : part * 128 + 128] for at in (i, 2 + i))
                if not forward:
                    one, two = jnp.where(even, two, one), jnp.where(even, one, two)
                to_near[i, t, part] = one.astype(to_near.dtype)
                to_far[i, t, part] = two.astype(to_far.dtype)

    both_ways(coef, to_near.shape[1], run)


def sent(first, forward, shape, sources, left, right, coef):
    tiles = shape[1]
    arrays, places, count = flat(*sources)
    return pl.pallas_call(
        functools.partial(sent_kernel, first, forward, places, count),
        out_shape=(pltpu.VMEM(shape, jnp.bfloat16), pltpu.VMEM(shape, jnp.bfloat16)),
        in_specs=vmem_specs(count + 3),
        out_specs=tuple(vmem_specs(2)),
        scratch_shapes=scratch(tiles, 4),
        compiler_params=pltpu.CompilerParams(vmem_limit_bytes=GRANT),
        cost_estimate=pl.CostEstimate(flops=1_200_000_000 * tiles, bytes_accessed=4_000_000 * tiles, transcendentals=0),
        name="sent",
    )(*map(in_vmem, (*arrays, left, right, coef)))


def kept_kernel(places, count, *refs):
    (sources_a, sources_b), rest = places(refs[:count]), refs[count:]
    left, right, coef, own_a, own_b, mixed_a, product_a, mixed_b, product_b = rest
    half = own_a.shape[1]

    def run(first, forward, items, sources, out, mixed, product, t, steps):
        mix(t, forward, steps, (0, 1, 2), items, sources, coef, None, mixed)
        term = multiply(t, first, 2, left, right, mixed, product)
        for i in range(2):
            for part in range(2):
                out[i, t, part] = term[i * 128 : i * 128 + 128, part * 128 : part * 128 + 128]

    both_ways(coef, half, functools.partial(run, 0, True, KEPT_IN, sources_a, own_a, mixed_a, product_a))
    both_ways(coef, own_b.shape[1], functools.partial(run, half, False, KEPT_OUT, sources_b, own_b, mixed_b, product_b))


def kept(shape_a, shape_b, sources_a, sources_b, left, right, coef):
    arrays, places, count = flat(sources_a, sources_b)
    return pl.pallas_call(
        functools.partial(kept_kernel, places, count),
        out_shape=(pltpu.VMEM(shape_a, jnp.float32), pltpu.VMEM(shape_b, jnp.float32)),
        in_specs=vmem_specs(count + 3),
        out_specs=tuple(vmem_specs(2)),
        scratch_shapes=scratch(shape_a[1], 2) + scratch(shape_b[1], 2),
        compiler_params=pltpu.CompilerParams(vmem_limit_bytes=GRANT),
        cost_estimate=pl.CostEstimate(flops=2_400_000_000, bytes_accessed=8_000_000, transcendentals=0),
        name="kept",
    )(*map(in_vmem, (*arrays, left, right, coef)))


def gather_kernel(far, near, coef, out):
    inner = jnp.broadcast_to(coef[INNER][:1] > 0.5, out.shape[-2:])
    for index in itertools.product(*map(range, out.shape[:-2])):
        out[index] = near[index].astype(jnp.float32) + jnp.where(inner, far[index].astype(jnp.float32), 0.0)


def gather(near, far, coef):
    return pl.pallas_call(
        gather_kernel,
        out_shape=pltpu.VMEM(near.shape, jnp.float32),
        in_specs=vmem_specs(3),
        out_specs=vmem_specs(1)[0],
        compiler_params=pltpu.CompilerParams(vmem_limit_bytes=GRANT),
        cost_estimate=pl.CostEstimate(flops=1000_000_000, bytes_accessed=1000_000, transcendentals=0),
        name="gather",
    )(in_vmem(far), in_vmem(near), in_vmem(coef))


def finish_kernel(own_a, near_a, far_a, own_b, from_b, out, held, sems):
    tiles_a, tiles_b = own_a.shape[1], own_b.shape[1]
    f32 = jnp.float32
    copies = []
    for t in range(tiles_a + tiles_b):
        if t < tiles_a:
            value = own_a[:, t] + near_a[:, t].astype(f32) + far_a[:, t].astype(f32)
        else:
            value = own_b[:, t - tiles_a] + from_b[:, t - tiles_a]
        held[:, t] = value.astype(held.dtype)
        copies.append(pltpu.make_async_copy(held.at[:, t], out.at[0, :, t], sems.at[t]))
        copies[-1].start()
    for copy in copies:
        copy.wait()


def finish(own_a, near_a, far_a, own_b, from_b):
    e, tiles_a = own_a.shape[:2]
    tiles = tiles_a + own_b.shape[1]
    shape = (e, tiles) + own_a.shape[2:]
    return pl.pallas_call(
        finish_kernel,
        out_shape=jax.ShapeDtypeStruct((1,) + shape, jnp.bfloat16),
        in_specs=vmem_specs(5),
        out_specs=pl.BlockSpec(memory_space=pl.ANY),
        scratch_shapes=[pltpu.VMEM(shape, jnp.bfloat16), pltpu.SemaphoreType.DMA((tiles,))],
        compiler_params=pltpu.CompilerParams(vmem_limit_bytes=GRANT),
        name="finish",
    )(*map(in_vmem, (own_a, near_a, far_a, own_b, from_b)))


def choose_kernel(own, near, coef, out):
    first = jnp.broadcast_to(coef[OWN_ON][:1] > 0.5, out.shape[-2:])
    for index in itertools.product(*map(range, out.shape[:-2])):
        mine, other = own[index].astype(jnp.float32), near[index].astype(jnp.float32)
        out[index] = jnp.where(first, mine, other).astype(out.dtype)


def choose(own, near, coef):
    return pl.pallas_call(
        choose_kernel,
        out_shape=pltpu.VMEM(own.shape, own.dtype),
        in_specs=vmem_specs(3),
        out_specs=vmem_specs(1)[0],
        compiler_params=pltpu.CompilerParams(vmem_limit_bytes=GRANT),
        name="choose",
    )(in_vmem(own), in_vmem(near), in_vmem(coef))


def split_kernel(source, *refs):
    outs, sems = refs[:-1], refs[-1]
    copies, tile = [], 0
    for at, out in enumerate(outs):
        copies.append(pltpu.make_async_copy(source.at[0, :, pl.ds(tile, out.shape[1])], out, sems.at[at]))
        copies[-1].start()
        tile += out.shape[1]
    for copy in copies:
        copy.wait()


def split(tiles, counts):
    _, e, _, *rest = tiles.shape
    return pl.pallas_call(
        split_kernel,
        out_shape=tuple(pltpu.VMEM((e, count, *rest), tiles.dtype) for count in counts),
        in_specs=[pl.BlockSpec(memory_space=pltpu.HBM)],
        out_specs=tuple(vmem_specs(len(counts))),
        scratch_shapes=[pltpu.SemaphoreType.DMA((len(counts),))],
        compiler_params=pltpu.CompilerParams(vmem_limit_bytes=GRANT),
        name="split",
    )(in_hbm(tiles))


def local(green_tiles, dham_blocks, phonon_weight, phonon_modes, tile_pattern):
    n_e, n_k = (lax.axis_size(axis) for axis in AXES)
    route = routes(n_e, n_k)

    def send(block, name):
        return lax.ppermute(block, AXES, route[name])

    tiles = green_tiles[0]
    half = tiles.shape[1] // 2
    e_count, tile_count, *rest = tiles.shape
    shape_a, shape_b = (e_count, half, *rest), (e_count, tile_count - half, *rest)
    *in_a, in_b = split(green_tiles, [1] * half + [tile_count - half])
    e, k = (lax.axis_index(axis) for axis in AXES)
    inner = (e > 0) & (e < n_e - 1)
    parity = jnp.stack([e % 2, k % 2, inner, (e == 1) | (e == n_e - 2)]).astype(jnp.int32)
    near_a = [send(block, "pair") for block in in_a]
    far_b = send(in_b, "far")
    near_b = send(in_b, "core")
    left, right, coef, wide = prepare(parity, phonon_modes.T, phonon_weight.transpose(1, 2, 0), tile_pattern.T, dham_blocks)
    partial_b = premix(shape_b[1], in_b, coef)
    near_a[0], partial_b = lax.optimization_barrier((near_a[0], partial_b))
    cut = half // 2
    far_a = [send(choose(own, near, coef), "relay") for own, near in zip(in_a[:cut], near_a[:cut])]
    far_a += [send(near, "ring") for near in near_a[cut:]]
    far_b, near_a = lax.optimization_barrier((far_b, near_a))
    pair_b, cross_b = sent(half, False, shape_b, (near_b, far_b, partial_b), left, right, coef)
    cross_b = send(cross_b, "cross")
    pair_b = send(pair_b, "pair")
    core_a, next_a = sent(0, True, shape_a, (in_a, near_a, far_a, wide), left, right, coef)
    in_b, next_a = lax.optimization_barrier((in_b, next_a))
    core_a = send(core_a, "core")
    next_a = send(next_a, "far")
    own_a, own_b = kept(shape_a, shape_b, (in_a, near_a, far_a), (in_b, near_b, far_b), left, right, coef)
    own_b, pair_b = lax.optimization_barrier((own_b, pair_b))
    return finish(own_a, core_a, next_a, own_b, gather(pair_b, cross_b, coef))


def solution(mesh):
    placed = (P("momentum", "energy", None, None, None, None), P(), P(), P(), P())
    return jax.shard_map(
        local,
        mesh=mesh,
        in_specs=placed,
        out_specs=P("momentum", "energy", None, None, None, None),
        check_vma=False,
    )
```

```python
import functools
import itertools
import jax
import jax.numpy as jnp
from jax import lax
from jax.experimental import pallas as pl
from jax.experimental.pallas import tpu as pltpu
from jax.sharding import PartitionSpec as P

AXES = ("energy", "momentum")
DIRS = 3
REACH = 2
EVEN = 3 * DIRS * (2 * REACH + 1)
AT_REST = EVEN + 1
INNER = EVEN + 2
OWN_ON = EVEN + 3
ENTRIES = EVEN + 4
ROWS = 32
GRANT = 16 * 2**20


def in_vmem(array):
    return pltpu.with_memory_space_constraint(array, pltpu.VMEM)


def in_hbm(array):
    return pltpu.with_memory_space_constraint(array, pltpu.HBM)


def vmem_specs(count):
    return [pl.BlockSpec(memory_space=pltpu.VMEM)] * count


def routes(n_e, n_k):
    def pairs(step):
        return [(e * n_k + k, to_e * n_k + to_k % n_k) for e in range(n_e) for k in range(n_k) for to_e, to_k in [step(e, k)]]

    def relay(e, k):
        if e in (0, n_e - 1):
            return e, k ^ 1
        if e in (1, n_e - 2):
            return (2 if e == 1 else n_e - 3), k
        return e + 2 - 4 * (e % 2), k

    def ring(e, k):
        to_e = e + 2 - 4 * (e % 2)
        return (to_e if 0 <= to_e < n_e else e ^ 1), k

    def cross(e, k):
        to_e = e - 1 + 2 * (e % 2)
        return (to_e, k) if 0 <= to_e < n_e else (e, k ^ 1)

    return {
        "pair": pairs(lambda e, k: (e ^ 1, k)),
        "relay": pairs(relay),
        "ring": pairs(ring),
        "cross": pairs(cross),
        "core": pairs(lambda e, k: (e, k ^ 1)),
        "far": pairs(lambda e, k: (e, k - 1 + 2 * (k % 2))),
    }


def prepare_kernel(parity, modes, weight, pattern, dham, left, right, coef, table):
    mode_count = modes.shape[1]
    tile_count = pattern.shape[1]
    for q in range(4):
        for d in range(DIRS):
            for s in range(2 * REACH + 1):
                table[q, d, s] = 0.0
    for m in range(mode_count):
        q = modes[0, m] + 1
        step = modes[1, m]
        for d in range(DIRS):
            table[q, d, REACH - step] = table[q, d, REACH - step] + weight[d, 0, m]
            table[q, d, REACH + step] = table[q, d, REACH + step] + weight[d, 1, m]
    toward = 1 - 2 * parity[1]
    at_rest = 0.0
    for slot, q in enumerate((0, toward, -toward)):
        for d in range(DIRS):
            for s in range(2 * REACH + 1):
                value = table[q + 1, d, s]
                if s == REACH:
                    at_rest = at_rest + jnp.abs(value)
                value = jnp.full((8, 128), value, jnp.float32)
                coef[(slot * DIRS + d) * (2 * REACH + 1) + s] = value.astype(jnp.bfloat16).astype(jnp.float32)
    coef[EVEN] = jnp.full((8, 128), 1 - parity[0], jnp.int32).astype(jnp.float32)
    coef[INNER] = jnp.full((8, 128), parity[2], jnp.int32).astype(jnp.float32)
    coef[OWN_ON] = jnp.full((8, 128), parity[3], jnp.int32).astype(jnp.float32)
    coef[AT_REST] = jnp.full((8, 128), at_rest, jnp.float32)
    for t in range(tile_count):
        lo, hi = pattern[0, t], pattern[1, t]
        for d in range(DIRS):
            real, imag = dham[d, lo, 0], dham[d, lo, 1]
            left[t, d, :128, :128] = real
            left[t, d, :128, 128:] = -imag
            left[t, d, 128:, :128] = imag
            left[t, d, 128:, 128:] = real
            real, imag = dham[d, hi, 0].T, dham[d, hi, 1].T
            right[t, d, :128, :128] = real
            right[t, d, :128, 128:] = -imag
            right[t, d, 128:, :128] = imag
            right[t, d, 128:, 128:] = real


def prepare(parity, modes, weight, pattern, dham):
    tile_count = pattern.shape[1]
    big = pltpu.VMEM((tile_count, DIRS, 256, 256), jnp.bfloat16)
    return pl.pallas_call(
        prepare_kernel,
        out_shape=(big, big, pltpu.VMEM((ENTRIES, 8, 128), jnp.float32)),
        in_specs=[pl.BlockSpec(memory_space=pltpu.SMEM)] * 4 + vmem_specs(1),
        out_specs=tuple(vmem_specs(3)),
        scratch_shapes=[pltpu.SMEM((4, DIRS, 2 * REACH + 1), jnp.float32)],
        compiler_params=pltpu.CompilerParams(vmem_limit_bytes=GRANT),
        name="prepare",
    )(parity, in_hbm(modes), in_hbm(weight), in_hbm(pattern), in_hbm(dham))


def mix(t, forward, steps, blocks, items, sources, coef, partial, out):
    even, inner = coef[EVEN] > 0.5, coef[INNER] > 0.5

    def at(slot, d, s):
        return coef[(slot * DIRS + d) * (2 * REACH + 1) + s + REACH]

    for part in range(2):
        for row in range(0, 128, ROWS):

            def load(source, j):
                ref, tile = (source[t], 0) if isinstance(source, list) else (source, t)
                return ref[j, tile, part, pl.ds(row, ROWS), :].astype(jnp.float32).reshape(ROWS // 8, 8, 128)

            taken = {block: [load(sources[block], j) for j in range(2)] for block in blocks}
            if forward:
                taken[2] = [jnp.where(inner, value, 0.0) for value in taken[2]]
                below = [jnp.where(even, b, a) for a, b in zip(taken[1], taken[2])]
                above = [jnp.where(even, a, b) for a, b in zip(taken[1], taken[2])]
                line = below + taken[0] + above
            for d in range(DIRS):
                for at_item, item in enumerate(items):
                    if forward:
                        slot, i = divmod(item, 2)
                        terms = [(line[2 + i + s], at(slot, d, s)) for s in steps]
                    else:
                        place = item - 2
                        terms = [(taken[m][j], at((0, 2, 1)[m], d, j - place)) for m in blocks for j in range(2) if j - place in steps]
                    here = (t, d, pl.ds(part * 128 + row, ROWS), pl.ds(at_item * 128, 128))
                    acc = terms[0][0] * terms[0][1]
                    if partial is not None:
                        acc = acc + partial[here].reshape(ROWS // 8, 8, 128)
                    for value, factor in terms[1:]:
                        acc = acc + value * factor
                    out[here] = acc.reshape(ROWS, 128).astype(out.dtype)


def multiply(t, first, count, left, right, mixed, product):
    for d in range(DIRS):
        got = jnp.dot(left[first + t, d], mixed[t, d], preferred_element_type=jnp.float32).astype(jnp.bfloat16)
        for item in range(count):
            for part in range(2):
                product[t, pl.ds(item * 128, 128), pl.ds(d * 256 + part * 128, 128)] = got[
                    part * 128 : part * 128 + 128, item * 128 : item * 128 + 128
                ]
    return jnp.dot(product[t], right[first + t].reshape(DIRS * 256, 256), preferred_element_type=jnp.float32)


def both_ways(coef, tiles, run):
    at_rest = jnp.max(coef[AT_REST])

    @pl.when(at_rest == 0.0)
    def _():
        for t in range(tiles):
            run(t, (-2, -1, 1, 2))

    @pl.when(at_rest != 0.0)
    def _():
        for t in range(tiles):
            run(t, (-2, -1, 0, 1, 2))


def flat(*sources):
    arrays, places = jax.tree.flatten(sources)
    return arrays, functools.partial(jax.tree.unflatten, places), len(arrays)


def scratch(tiles, count):
    return [
        pltpu.VMEM((tiles, DIRS, 256, count * 128), jnp.bfloat16),
        pltpu.VMEM((tiles, count * 128, DIRS * 256), jnp.bfloat16),
    ]


SENT_IN, SENT_OUT, KEPT_IN, KEPT_OUT = (2, 3, 4, 5), (0, 1, 4, 5), (0, 1), (2, 3)


def premix_kernel(places, count, *refs):
    (own,), (coef, partial) = places(refs[:count]), refs[count:]
    both_ways(coef, partial.shape[0], lambda t, steps: mix(t, False, steps, (0,), SENT_OUT, (own,), coef, None, partial))


def premix(tiles, own, coef):
    arrays, places, count = flat(own)
    return pl.pallas_call(
        functools.partial(premix_kernel, places, count),
        out_shape=pltpu.VMEM((tiles, DIRS, 256, len(SENT_OUT) * 128), jnp.float32),
        in_specs=vmem_specs(count + 1),
        out_specs=vmem_specs(1)[0],
        compiler_params=pltpu.CompilerParams(vmem_limit_bytes=GRANT),
        cost_estimate=pl.CostEstimate(flops=300_000_000 * tiles, bytes_accessed=1_000_000 * tiles, transcendentals=0),
        name="premix",
    )(*map(in_vmem, (*arrays, coef)))


def sent_kernel(first, forward, places, count, *refs):
    sources, (left, right, coef, to_near, to_far, mixed, product) = places(refs[:count]), refs[count:]

    def run(t, steps):
        if forward:
            mix(t, True, steps, (0, 1, 2), SENT_IN, sources, coef, None, mixed)
        else:
            mix(t, False, steps, (1, 2), SENT_OUT, {1: sources[0], 2: sources[1]}, coef, sources[2], mixed)
        term = multiply(t, first, 4, left, right, mixed, product)
        even = jnp.broadcast_to(coef[EVEN][:1] > 0.5, (128, 128))
        for i in range(2):
            for part in range(2):
                one, two = (term[at * 128 : at * 128 + 128, part * 128 : part * 128 + 128] for at in (i, 2 + i))
                if not forward:
                    one, two = jnp.where(even, two, one), jnp.where(even, one, two)
                to_near[i, t, part] = one.astype(to_near.dtype)
                to_far[i, t, part] = two.astype(to_far.dtype)

    both_ways(coef, to_near.shape[1], run)


def sent(first, forward, shape, sources, left, right, coef):
    tiles = shape[1]
    arrays, places, count = flat(*sources)
    return pl.pallas_call(
        functools.partial(sent_kernel, first, forward, places, count),
        out_shape=(pltpu.VMEM(shape, jnp.bfloat16), pltpu.VMEM(shape, jnp.bfloat16)),
        in_specs=vmem_specs(count + 3),
        out_specs=tuple(vmem_specs(2)),
        scratch_shapes=scratch(tiles, 4),
        compiler_params=pltpu.CompilerParams(vmem_limit_bytes=GRANT),
        cost_estimate=pl.CostEstimate(flops=1_200_000_000 * tiles, bytes_accessed=4_000_000 * tiles, transcendentals=0),
        name="sent",
    )(*map(in_vmem, (*arrays, left, right, coef)))


def kept_kernel(places, count, *refs):
    (sources_a, sources_b), rest = places(refs[:count]), refs[count:]
    left, right, coef, own_a, own_b, mixed_a, product_a, mixed_b, product_b = rest
    half = own_a.shape[1]

    def run(first, forward, items, sources, out, mixed, product, t, steps):
        mix(t, forward, steps, (0, 1, 2), items, sources, coef, None, mixed)
        term = multiply(t, first, 2, left, right, mixed, product)
        for i in range(2):
            for part in range(2):
                out[i, t, part] = term[i * 128 : i * 128 + 128, part * 128 : part * 128 + 128]

    both_ways(coef, half, functools.partial(run, 0, True, KEPT_IN, sources_a, own_a, mixed_a, product_a))
    both_ways(coef, own_b.shape[1], functools.partial(run, half, False, KEPT_OUT, sources_b, own_b, mixed_b, product_b))


def kept(shape_a, shape_b, sources_a, sources_b, left, right, coef):
    arrays, places, count = flat(sources_a, sources_b)
    return pl.pallas_call(
        functools.partial(kept_kernel, places, count),
        out_shape=(pltpu.VMEM(shape_a, jnp.float32), pltpu.VMEM(shape_b, jnp.float32)),
        in_specs=vmem_specs(count + 3),
        out_specs=tuple(vmem_specs(2)),
        scratch_shapes=scratch(shape_a[1], 2) + scratch(shape_b[1], 2),
        compiler_params=pltpu.CompilerParams(vmem_limit_bytes=GRANT),
        cost_estimate=pl.CostEstimate(flops=2_400_000_000, bytes_accessed=8_000_000, transcendentals=0),
        name="kept",
    )(*map(in_vmem, (*arrays, left, right, coef)))


def gather_kernel(far, near, coef, out):
    inner = jnp.broadcast_to(coef[INNER][:1] > 0.5, out.shape[-2:])
    for index in itertools.product(*map(range, out.shape[:-2])):
        out[index] = near[index].astype(jnp.float32) + jnp.where(inner, far[index].astype(jnp.float32), 0.0)


def gather(near, far, coef):
    return pl.pallas_call(
        gather_kernel,
        out_shape=pltpu.VMEM(near.shape, jnp.float32),
        in_specs=vmem_specs(3),
        out_specs=vmem_specs(1)[0],
        compiler_params=pltpu.CompilerParams(vmem_limit_bytes=GRANT),
        cost_estimate=pl.CostEstimate(flops=1000_000_000, bytes_accessed=1000_000, transcendentals=0),
        name="gather",
    )(in_vmem(far), in_vmem(near), in_vmem(coef))


def finish_kernel(own_a, near_a, far_a, own_b, from_b, out, held, sems):
    tiles_a, tiles_b = own_a.shape[1], own_b.shape[1]
    f32 = jnp.float32
    copies = []
    for t in range(tiles_a + tiles_b):
        if t < tiles_a:
            value = own_a[:, t] + near_a[:, t].astype(f32) + far_a[:, t].astype(f32)
        else:
            value = own_b[:, t - tiles_a] + from_b[:, t - tiles_a]
        for e in range(held.shape[0]):
            held[e, t] = value[e].astype(held.dtype)
            copies.append(pltpu.make_async_copy(held.at[e, t], out.at[0, e, t], sems.at[len(copies)]))
            copies[-1].start()
    for copy in copies:
        copy.wait()


def finish(own_a, near_a, far_a, own_b, from_b):
    e, tiles_a = own_a.shape[:2]
    tiles = tiles_a + own_b.shape[1]
    shape = (e, tiles) + own_a.shape[2:]
    return pl.pallas_call(
        finish_kernel,
        out_shape=jax.ShapeDtypeStruct((1,) + shape, jnp.bfloat16),
        in_specs=vmem_specs(5),
        out_specs=pl.BlockSpec(memory_space=pl.ANY),
        scratch_shapes=[pltpu.VMEM(shape, jnp.bfloat16), pltpu.SemaphoreType.DMA((e * tiles,))],
        compiler_params=pltpu.CompilerParams(vmem_limit_bytes=GRANT),
        name="finish",
    )(*map(in_vmem, (own_a, near_a, far_a, own_b, from_b)))


def choose_kernel(own, near, coef, out):
    first = jnp.broadcast_to(coef[OWN_ON][:1] > 0.5, out.shape[-2:])
    for index in itertools.product(*map(range, out.shape[:-2])):
        mine, other = own[index].astype(jnp.float32), near[index].astype(jnp.float32)
        out[index] = jnp.where(first, mine, other).astype(out.dtype)


def choose(own, near, coef):
    return pl.pallas_call(
        choose_kernel,
        out_shape=pltpu.VMEM(own.shape, own.dtype),
        in_specs=vmem_specs(3),
        out_specs=vmem_specs(1)[0],
        compiler_params=pltpu.CompilerParams(vmem_limit_bytes=GRANT),
        name="choose",
    )(in_vmem(own), in_vmem(near), in_vmem(coef))


def split_kernel(source, *refs):
    outs, sems = refs[:-1], refs[-1]
    copies, tile = [], 0
    for at, out in enumerate(outs):
        copies.append(pltpu.make_async_copy(source.at[0, :, pl.ds(tile, out.shape[1])], out, sems.at[at]))
        copies[-1].start()
        tile += out.shape[1]
    for copy in copies:
        copy.wait()


def split(tiles, counts):
    _, e, _, *rest = tiles.shape
    return pl.pallas_call(
        split_kernel,
        out_shape=tuple(pltpu.VMEM((e, count, *rest), tiles.dtype) for count in counts),
        in_specs=[pl.BlockSpec(memory_space=pltpu.HBM)],
        out_specs=tuple(vmem_specs(len(counts))),
        scratch_shapes=[pltpu.SemaphoreType.DMA((len(counts),))],
        compiler_params=pltpu.CompilerParams(vmem_limit_bytes=GRANT),
        name="split",
    )(in_hbm(tiles))


def local(green_tiles, dham_blocks, phonon_weight, phonon_modes, tile_pattern):
    n_e, n_k = (lax.axis_size(axis) for axis in AXES)
    route = routes(n_e, n_k)

    def send(block, name):
        return lax.ppermute(block, AXES, route[name])

    tiles = green_tiles[0]
    half = tiles.shape[1] // 2
    e_count, tile_count, *rest = tiles.shape
    shape_a, shape_b = (e_count, half, *rest), (e_count, tile_count - half, *rest)
    *in_a, in_b = split(green_tiles, [1] * half + [tile_count - half])
    e, k = (lax.axis_index(axis) for axis in AXES)
    inner = (e > 0) & (e < n_e - 1)
    parity = jnp.stack([e % 2, k % 2, inner, (e == 1) | (e == n_e - 2)]).astype(jnp.int32)
    near_a = [send(block, "pair") for block in in_a]
    far_b = send(in_b, "far")
    near_b = send(in_b, "core")
    left, right, coef = prepare(parity, phonon_modes.T, phonon_weight.transpose(1, 2, 0), tile_pattern.T, dham_blocks)
    partial_b = premix(shape_b[1], in_b, coef)
    near_a[0], partial_b = lax.optimization_barrier((near_a[0], partial_b))
    cut = half // 2
    far_a = [send(choose(own, near, coef), "relay") for own, near in zip(in_a[:cut], near_a[:cut])]
    far_a += [send(near, "ring") for near in near_a[cut:]]
    far_b, near_a = lax.optimization_barrier((far_b, near_a))
    pair_b, cross_b = sent(half, False, shape_b, (near_b, far_b, partial_b), left, right, coef)
    cross_b = send(cross_b, "cross")
    pair_b = send(pair_b, "pair")
    core_a, next_a = sent(0, True, shape_a, (in_a, near_a, far_a), left, right, coef)
    in_b, next_a = lax.optimization_barrier((in_b, next_a))
    core_a = send(core_a, "core")
    next_a = send(next_a, "far")
    own_a, own_b = kept(shape_a, shape_b, (in_a, near_a, far_a), (in_b, near_b, far_b), left, right, coef)
    own_b, pair_b = lax.optimization_barrier((own_b, pair_b))
    return finish(own_a, core_a, next_a, own_b, gather(pair_b, cross_b, coef))


def solution(mesh):
    placed = (P("momentum", "energy", None, None, None, None), P(), P(), P(), P())
    return jax.shard_map(
        local,
        mesh=mesh,
        in_specs=placed,
        out_specs=P("momentum", "energy", None, None, None, None),
        check_vma=False,
    )
```
